128 devices in a mesh: dp: 16 (over x, z), tensor: 8 (over y, core).
Axes of the slice: x: 4, y: 4, z: 4, core: 2. Of those that a mesh axis runs over, the one named last changes fastest.
Arguments:
- tokens: bfloat16 [16384, 2880], P(('dp', 'tensor'))
- positions: int32 [16, 1024], P('dp'), may hold values from 0 to 32767, as said below
- doc_ids: int32 [16, 1024], P('dp'), may hold values from 0 to 3, never falling along the last dimension, each value on 1 to 512 neighbouring positions
- w_query: bfloat16 [2880, 4096], P('dp', 'tensor')
- key_weight: bfloat16 [2880, 512], P('dp', 'tensor')
- value_weight: bfloat16 [2880, 512], P('dp', 'tensor'), may hold values from -0.109375 to 0.109375
- w_out: bfloat16 [4096, 2880], P('tensor', 'dp'), may hold values from -0.375 to 0.375
- attn_gain: float32 [2880], replicated, may hold values from 0.25 to 1.75
- moe_gain: float32 [2880], replicated, may hold values from 0.25 to 1.75
- expert_ids: int32 [16384, 4], P(('dp', 'tensor')), may hold values from 0 to 127, all different within a row; in each aligned block of 128 rows (0 to 127, 128 to 255, ...) at most 6 rows name the same one
- gate_weights: float32 [16384, 4], P(('dp', 'tensor')), may hold values from 0.1 to 1
- w_gate_up: bfloat16 [128, 2880, 2880], P(('dp', 'tensor')), may hold values from -0.109375 to 0.109375
- w_down: bfloat16 [128, 1440, 2880], P(('dp', 'tensor')), may hold values from -0.15625 to 0.15625
Outputs:
- mixed: bfloat16 [16384, 2880], P(('dp', 'tensor'))
The draws below stay inside these ranges and needn't reach their ends.
Inputs may be any that keep to these rules, and one draw needn't show every extreme that they name: Within a window the positions rise by one from 0, except for one jump forward at a point drawn per window; in some window the last position is 32767. `expert_ids`: A token names 4 different experts. In each aligned block of 128 rows (the rows of one device) no expert is named by more than 6 rows.
All inputs are finite; a program needn't handle non-finite values.
Results may differ from the reference program's by a relative error of at most 0.02.
The reference program's roundings to bfloat16 on the way count: a program that leaves them out, or rounds other values in their place, can miss the bound.
Values may be sent and summed in bfloat16 or wider, within the bound.
No kernel may reach another device: no remote copies, remote signals or barrier semaphores. Data moves between devices by JAX's collectives and lax.ppermute only.
A program may use at most 128 MiB of HBM per device.

```python
import math
import jax
import jax.numpy as jnp
import numpy as np
from jax import lax

MODEL_WIDTH = 2880
QUERY_HEADS = 64
KEY_VALUE_HEADS = 8
HEAD_SIZE = 64
TOP = 4
FF = 1440
MAXPOS = 32768
ROWS = 128
WINDOW_TOKENS = 1024
WINDOWS = 16
TOKENS = 16384
EXPERTS = 128
CAP = 6
N_TENSOR = 8


def query_base(key):
    return jax.random.normal(key, (MODEL_WIDTH, QUERY_HEADS * HEAD_SIZE), jnp.float32) / math.sqrt(MODEL_WIDTH)


def draw_tokens(key, part):
    key = jax.random.fold_in(key, 21)
    primary_key = jax.random.fold_in(key, 0)
    rotary_base = jax.random.normal(primary_key, (TOKENS, MODEL_WIDTH), jnp.float32)
    return jnp.clip(rotary_base, -6.0, 6.0).astype(jnp.bfloat16)


def draw_positions(key, part):
    key = jax.random.fold_in(key, 31)
    primary_key, secondary_key, third_key = jax.random.split(key, 3)
    split_at = jax.random.randint(primary_key, (WINDOWS, 1), 1, WINDOW_TOKENS)
    jump = jax.random.randint(secondary_key, (WINDOWS, 1), 0, MAXPOS - WINDOW_TOKENS + 1)
    widest = jax.random.randint(third_key, (), 0, WINDOWS)
    jump = jnp.where(jnp.arange(WINDOWS, dtype=jnp.int32)[:, None] == widest, MAXPOS - WINDOW_TOKENS, jump)
    index = jnp.arange(WINDOW_TOKENS, dtype=jnp.int32)[None, :]
    return (index + jnp.where(index >= split_at, jump, 0)).astype(jnp.int32)


def draw_w_query(key, part):
    rotary_base = query_base(key)
    return rotary_base.astype(jnp.bfloat16)


def draw_key_weight(key, part):
    key = jax.random.fold_in(key, 41)
    primary_key = jax.random.fold_in(key, 0)
    own_share = jax.random.normal(primary_key, (MODEL_WIDTH, KEY_VALUE_HEADS, HEAD_SIZE), jnp.float32) / math.sqrt(MODEL_WIDTH)
    return own_share.reshape(MODEL_WIDTH, KEY_VALUE_HEADS * HEAD_SIZE).astype(jnp.bfloat16)


def shard_levels(key, extent, cuts, least, high):
    factor_of, own = 1.0, jax.random.fold_in(key, 6)
    for dim, shards_of in cuts:
        steps = jnp.exp(jax.random.uniform(jax.random.fold_in(own, dim), (shards_of,), jnp.float32, least / len(cuts), high / len(cuts)))
        factor_of = factor_of * jnp.repeat(steps, extent[dim] // shards_of).reshape([-1 if axis == dim else 1 for axis in range(len(extent))])
    return factor_of


def length_profile(count, total, most, slope):
    loads = [(1 << 20) // math.isqrt(grade ** slope) + 1 for grade in range(2, count + 1)]
    spare, given = total - most - (count - 1), [1] * (count - 1)
    while spare > 0:
        free = [i for i in range(count - 1) if given[i] < most]
        mass, budget = sum([loads[i] for i in free]), spare
        for i in free:
            more = min(most - given[i], max(1, budget * loads[i] // mass), spare)
            given[i] = given[i] + more
            spare = spare - more
    return np.array([most] + given)


def ragged(rng, count, total, reach, skew):
    if count == 2:
        one = jax.random.randint(rng, (), max(1, total - reach), min(reach, total - 1) + 1)
        return jnp.stack([one, total - one])
    sizes = jnp.asarray(length_profile(count, total, reach, skew), jnp.int32)
    pairs = (count - 1) // 2
    giver, sink = sizes[1:1 + 2 * pairs:2], sizes[2:2 + 2 * pairs:2]
    room = jnp.minimum(giver - 1, reach - sink)
    passed = jax.random.randint(jax.random.fold_in(rng, 1), (pairs,), 0, 1 << 20) % (room + 1)
    sizes = sizes.at[1:1 + 2 * pairs:2].set(giver - passed).at[2:2 + 2 * pairs:2].set(sink + passed)
    return sizes[jax.random.permutation(jax.random.fold_in(rng, 2), count)]


def deal_out(own_key, own, number, rows, number_of, top, most, lean):
    sequence = jax.random.permutation(own_key, number_of)
    heavy_load, ordinary = portions_of(number_of, rows * top, most, lean, True), portions_of(number_of, rows * top, most, lean, False)
    places = jnp.arange(number_of)

    def named(sizes, turn):
        used = int((sizes > 0).sum())
        fixed = max(1, used // 4)
        moved = fixed + (places - fixed + turn * (used - fixed)) % max(1, number_of - fixed)
        return jnp.zeros((number_of,), jnp.int32).at[sequence[jnp.where(places < fixed, places, moved)]].set(jnp.asarray(sizes, jnp.int32))

    sizes = jnp.where(number % 4 == 0, named(heavy_load, number // 4), named(ordinary, number - number // 4 - 1))
    mixed = jax.random.permutation(jax.random.fold_in(own, 3), number_of)
    donor, taker = mixed[0:number_of // 2 * 2:2], mixed[1:number_of // 2 * 2:2]
    margin = jnp.minimum(sizes[donor] - 1, most - sizes[taker]) // 2
    margin = jnp.where((donor == sequence[0]) | (taker == sequence[0]) | (sizes[taker] == 0), 0, jnp.maximum(margin, 0))
    moved = jax.random.randint(jax.random.fold_in(own, 4), (number_of // 2,), 0, 1 << 20) % (margin + 1)
    sizes = sizes.at[donor].add(-moved).at[taker].add(moved)
    labels = jnp.searchsorted(jnp.cumsum(sizes), jnp.arange(rows * top), side="right").astype(jnp.int32)
    table = labels.reshape(top, rows).T
    table = table[jax.random.permutation(jax.random.fold_in(own, 1), rows)]
    turn = jax.random.randint(jax.random.fold_in(own, 2), (rows, 1), 0, top)
    return jnp.take_along_axis(table, (jnp.arange(top)[None, :] + turn) % top, axis=1)


def portions_of(amount, total, most, lean, full):
    weights = [(1 << 20) // math.isqrt(standing ** lean) + 1 for standing in range(1, amount + 1)]
    largest = most if full else min(most, max(-(-total // amount), total * weights[0] // sum(weights)))
    least = 1 if total - largest >= amount - 1 else 0
    given, surplus = [largest] + [least] * (amount - 1), total - largest - least * (amount - 1)
    while surplus > 0:
        free = [i for i in range(1, amount) if given[i] < largest] or [i for i in range(1, amount) if given[i] < most]
        whole, left = sum([weights[i] for i in free]), surplus
        for i in free:
            extra = min(most - given[i], max(1, left * weights[i] // whole), surplus)
            given[i] = given[i] + extra
            surplus = surplus - extra
    return np.array(given)


def bell_draw(key, shape, scale, reach, pieces=(), kind=jnp.bfloat16):
    array = jax.random.normal(key, shape, jnp.float32) * scale
    if len(pieces) > 0:
        array = shard_levels(key, shape, pieces, -0.22, 0.18) * array
    return jnp.clip(array, min=-reach, max=reach).astype(kind)


def setup_inputs(seed: int = 0) -> dict:
    streams_of = jax.random.split(jax.random.key(seed), 14)
    tokens = draw_tokens(jax.random.fold_in(streams_of[13], 71), 0)
    positions = draw_positions(jax.random.fold_in(streams_of[13], 71), 0)
    doc_ids = jax.vmap(lambda own: jnp.searchsorted(jnp.cumsum(ragged(own, 4, WINDOW_TOKENS, WINDOW_TOKENS // 2, 0)), jnp.arange(WINDOW_TOKENS), side="right"))(jax.random.split(streams_of[2], WINDOWS)).reshape((WINDOWS, WINDOW_TOKENS)).astype(jnp.int32)
    w_query = draw_w_query(jax.random.fold_in(streams_of[13], 71), 0)
    key_weight = draw_key_weight(jax.random.fold_in(streams_of[13], 71), 0)
    value_weight = bell_draw(streams_of[5], (MODEL_WIDTH, KEY_VALUE_HEADS * HEAD_SIZE), MODEL_WIDTH ** -0.5, 0.109375, ((0, 16), (1, 8)))
    w_out = bell_draw(streams_of[6], (QUERY_HEADS * HEAD_SIZE, MODEL_WIDTH), (QUERY_HEADS * HEAD_SIZE // 16) ** -0.5, 0.375, ((0, 8), (1, 16)))
    attn_gain = jnp.clip(1.0 + 0.15 * jax.random.normal(streams_of[7], (MODEL_WIDTH,), jnp.float32), 0.25, 1.75)
    moe_gain = jnp.clip(1.0 + 0.15 * jax.random.normal(streams_of[8], (MODEL_WIDTH,), jnp.float32), 0.25, 1.75)
    expert_ids_keys = jax.random.split(jax.random.fold_in(streams_of[9], 1), TOKENS // ROWS)
    expert_ids_turns = jax.random.permutation(jax.random.fold_in(streams_of[9], 3), TOKENS // ROWS)
    expert_ids = jax.vmap(lambda own, number: deal_out(jax.random.fold_in(streams_of[9], 2), own, number, ROWS, EXPERTS, TOP, CAP, 2))(expert_ids_keys, expert_ids_turns).reshape((TOKENS, TOP))
    gate_weights = jnp.clip(0.1 + 0.9 * jax.random.uniform(streams_of[10], (TOKENS, TOP), jnp.float32) ** shard_levels(streams_of[10], (TOKENS, TOP), ((0, 128),), -0.2, 0.2), 0.1, 1.0)
    w_gate_up = bell_draw(streams_of[11], (EXPERTS, MODEL_WIDTH, 2 * FF), MODEL_WIDTH ** -0.5, 0.109375, ((0, 128),))
    w_down = bell_draw(streams_of[12], (EXPERTS, FF, MODEL_WIDTH), FF ** -0.5, 0.15625, ((0, 128),))
    return dict(tokens=tokens, positions=positions, doc_ids=doc_ids, w_query=w_query, key_weight=key_weight, value_weight=value_weight, w_out=w_out, attn_gain=attn_gain, moe_gain=moe_gain, expert_ids=expert_ids, gate_weights=gate_weights, w_gate_up=w_gate_up, w_down=w_down)


def rms_norm(value_rows, gain):
    mean_square = lax.optimization_barrier(jnp.mean(value_rows * value_rows, axis=-1, keepdims=True))
    return value_rows * lax.rsqrt(mean_square + 1e-05) * gain

def rotate(value_rows, position):
    half = value_rows.shape[-1] // 2
    freq = jnp.exp(jnp.arange(half, dtype=jnp.float32) * (-2.0 * math.log(150000.0) / value_rows.shape[-1]))
    angle = position.astype(jnp.float32)[:, None] * freq[None, :]
    cosine = jnp.cos(angle)[:, None, :]
    sine = jnp.sin(angle)[:, None, :]
    first = value_rows[..., :half]
    second = value_rows[..., half:]
    return jnp.concatenate([first * cosine - second * sine, second * cosine + first * sine], axis=-1)

def attend_group(query_group, key_head, value_head, allowed):
    scores = jnp.einsum('gqd,kd->gqk', query_group.astype(jnp.float32), key_head.astype(jnp.float32))
    scores = scores * HEAD_SIZE ** (-0.5)
    masked = jnp.where(allowed[None], scores, -1e+30)
    largest = lax.optimization_barrier(jnp.max(masked, axis=-1, keepdims=True))
    weights = jnp.where(allowed[None], jnp.exp(masked - largest), 0.0)
    probs = (weights / lax.optimization_barrier(jnp.sum(weights, axis=-1, keepdims=True))).astype(jnp.bfloat16)
    mixed = jnp.einsum('gqk,kd->gqd', probs.astype(jnp.float32), value_head.astype(jnp.float32))
    return mixed.astype(jnp.bfloat16)

def reference(tokens, positions, doc_ids, w_query, key_weight, value_weight, w_out, attn_gain, moe_gain, expert_ids, gate_weights, w_gate_up, w_down):
    resid_in = tokens.astype(jnp.float32)
    normed = rms_norm(resid_in, attn_gain).astype(jnp.bfloat16)
    head_group = QUERY_HEADS // KEY_VALUE_HEADS

    def one_window(packed):
        token_rows, position, docs = packed
        query_rows = jnp.dot(token_rows, w_query, preferred_element_type=jnp.float32).reshape(WINDOW_TOKENS, QUERY_HEADS, HEAD_SIZE)
        key_rows = jnp.dot(token_rows, key_weight, preferred_element_type=jnp.float32).reshape(WINDOW_TOKENS, KEY_VALUE_HEADS, HEAD_SIZE)
        value_rows = jnp.dot(token_rows, value_weight, preferred_element_type=jnp.float32).reshape(WINDOW_TOKENS, KEY_VALUE_HEADS, HEAD_SIZE)
        query_rows = rotate(query_rows, position).astype(jnp.bfloat16)
        key_rows = rotate(key_rows, position).astype(jnp.bfloat16)
        value_rows = value_rows.astype(jnp.bfloat16)
        index = jnp.arange(WINDOW_TOKENS, dtype=jnp.int32)
        allowed = (index[:, None] >= index[None, :]) & (docs[:, None] == docs[None, :])
        grouped_heads = query_rows.reshape(WINDOW_TOKENS, KEY_VALUE_HEADS, head_group, HEAD_SIZE).transpose(1, 2, 0, 3)

        def one_head(parts):
            return attend_group(parts[0], parts[1], parts[2], allowed)
        mixed = lax.map(one_head, (grouped_heads, key_rows.transpose(1, 0, 2), value_rows.transpose(1, 0, 2)))
        return mixed.transpose(2, 0, 1, 3).reshape(WINDOW_TOKENS, QUERY_HEADS * HEAD_SIZE)
    heads = lax.map(one_window, (normed.reshape(WINDOWS, WINDOW_TOKENS, MODEL_WIDTH), positions, doc_ids)).reshape(TOKENS, QUERY_HEADS * HEAD_SIZE)
    columns = QUERY_HEADS * HEAD_SIZE // N_TENSOR
    attn_out = jnp.zeros((TOKENS, MODEL_WIDTH), jnp.float32)
    for part in range(N_TENSOR):
        term = jnp.dot(heads[:, part * columns:(part + 1) * columns], w_out[part * columns:(part + 1) * columns], preferred_element_type=jnp.float32)
        attn_out = attn_out + term.astype(jnp.bfloat16).astype(jnp.float32)
    resid = resid_in + attn_out
    moe_in = rms_norm(resid, moe_gain).astype(jnp.bfloat16)
    share = gate_weights / lax.optimization_barrier(jnp.sum(gate_weights, axis=-1, keepdims=True))
    bound = WINDOWS * N_TENSOR * CAP

    def one_expert(total, packed):
        expert, gate_up, down = packed
        hit = expert_ids == expert
        weight = lax.optimization_barrier(jnp.sum(jnp.where(hit, share, 0.0), axis=-1))
        chosen = jnp.any(hit, axis=-1)
        count = jnp.sum(chosen.astype(jnp.int32))
        picked = jnp.nonzero(chosen, size=bound, fill_value=0)[0].astype(jnp.int32)
        valid = jnp.arange(bound, dtype=jnp.int32) < count
        token_rows = moe_in[picked]
        both = jnp.dot(token_rows, gate_up, preferred_element_type=jnp.float32)
        gate = both[:, :FF]
        up = both[:, FF:]
        act = (gate * jax.nn.sigmoid(1.702 * gate) * (up + 1.0)).astype(jnp.bfloat16)
        result = jnp.dot(act, down, preferred_element_type=jnp.float32).astype(jnp.bfloat16).astype(jnp.float32)
        scale = jnp.where(valid, weight[picked], 0.0)
        return (total.at[picked].add(result * scale[:, None]), None)
    start = jnp.zeros((TOKENS, MODEL_WIDTH), jnp.float32)
    moe_out, unused = lax.scan(one_expert, start, (jnp.arange(EXPERTS, dtype=jnp.int32), w_gate_up, w_down))
    return (resid + moe_out).astype(jnp.bfloat16)
```

```python
import math

import jax
import jax.numpy as jnp
from jax import lax
from jax.experimental import pallas as pl
from jax.experimental.pallas import tpu as pltpu
from jax.sharding import PartitionSpec as P

HEAD = 64
WIDTH = 2880
FF = 1440
CAP = 6
SLOTS = 8
MAIN = 2304
TAIL = WIDTH - MAIN
STEP = 640
BF = jnp.bfloat16
F32 = jnp.float32
NT = (((1,), (1,)), ((), ()))
TN = (((0,), (0,)), ((), ()))
VMEM = pl.BlockSpec(memory_space=pltpu.VMEM)
ANY = pl.BlockSpec(memory_space=pl.ANY)


def rms_norm(value_rows, gain):
    mean_square = jnp.mean(value_rows * value_rows, axis=-1, keepdims=True)
    return value_rows * lax.rsqrt(mean_square + 1e-05) * gain


def attend_kernel(x_ref, w_ref, cos_ref, sin_ref, docq_ref, dock_ref, out_ref, q_buf, k_buf, v_buf):
    block = pl.program_id(0)
    rows = x_ref.shape[0]
    length = k_buf.shape[0] // 2
    base = pl.multiple_of(block * rows, rows)
    here = pl.ds(base, rows)

    projected = jnp.dot(x_ref[...], w_ref[...], preferred_element_type=F32)
    lanes = lax.broadcasted_iota(jnp.int32, (rows, 128), 1)
    low = (lanes % HEAD) < HEAD // 2
    cosine = cos_ref[...]
    sine = sin_ref[...]

    def turn(pair):
        swapped = jnp.where(
            low, pltpu.roll(pair, 128 - HEAD // 2, 1), pltpu.roll(pair, HEAD // 2, 1)
        )
        return pair * cosine + swapped * sine

    pairs = out_ref.shape[1] // 128
    for pair in range(pairs):
        cols = slice(pair * 128, pair * 128 + 128)
        q_buf[:, cols] = (turn(projected[:, cols]) * HEAD ** (-0.5)).astype(BF)
    key_value = projected[:, pairs * 128 :]
    turned = turn(key_value)
    first = lanes < HEAD
    crossed = pltpu.roll(key_value, HEAD, 1)
    turned_crossed = pltpu.roll(turned, HEAD, 1)
    one = jnp.ones((rows, 128), F32)
    zero = jnp.zeros((rows, 128), F32)
    k_buf[here, :] = jnp.where(first, turned, 0.0).astype(BF)
    k_buf[pl.ds(length + base, rows), :] = jnp.where(first, 0.0, turned_crossed).astype(BF)
    v_buf[here, 0:128] = jnp.where(first, crossed, zero).astype(BF)
    v_buf[here, 128:256] = jnp.where(first, one, zero).astype(BF)
    v_buf[pl.ds(length + base, rows), 0:128] = jnp.where(first, zero, key_value).astype(BF)
    v_buf[pl.ds(length + base, rows), 128:256] = jnp.where(first, zero, one).astype(BF)

    def attend(blocks):
        span = blocks * rows
        start = pl.multiple_of(base + rows - span, rows)
        window = pl.ds(start, span)
        other = pl.ds(length + start, span)
        docs = dock_ref[:, pl.ds(start, span)]
        row = lax.broadcasted_iota(jnp.int32, (rows, span), 0) + (span - rows)
        col = lax.broadcasted_iota(jnp.int32, (rows, span), 1)
        allowed = (row >= col) & (docq_ref[...] == docs)
        key_a, key_b = k_buf[window, :], k_buf[other, :]
        value_a, value_b = v_buf[window, :], v_buf[other, :]
        for pair in range(pairs):
            cols = slice(pair * 128, pair * 128 + 128)
            query = q_buf[:, cols]
            both = None
            for keys, values in ((key_a, value_a), (key_b, value_b)):
                scores = lax.dot_general(query, keys, NT, preferred_element_type=F32)
                scores = jnp.where(allowed, scores, -1e30)
                largest = jnp.max(scores, axis=-1, keepdims=True)
                weights = jnp.exp(scores - largest).astype(BF)
                part = jnp.dot(weights, values, preferred_element_type=F32)
                both = part if both is None else both + part
            out_ref[:, cols] = (both[:, :128] / both[:, 128:]).astype(BF)

    for blocks in range(1, 5):
        pl.when(block == blocks - 1)(lambda blocks=blocks: attend(blocks))
    pl.when(block >= 4)(lambda: attend(5))


def attend(x, w, cosine, sine, docs):
    length, width = x.shape
    columns = w.shape[1] - 2 * HEAD
    rows = 128
    return pl.pallas_call(
        attend_kernel,
        out_shape=jax.ShapeDtypeStruct((length, columns), BF),
        grid=(length // rows,),
        in_specs=[
            pl.BlockSpec((rows, width), lambda i: (i, 0)),
            pl.BlockSpec((width, w.shape[1]), lambda i: (0, 0)),
            pl.BlockSpec((rows, 128), lambda i: (i, 0)),
            pl.BlockSpec((rows, 128), lambda i: (i, 0)),
            pl.BlockSpec((rows, 1), lambda i: (i, 0)),
            pl.BlockSpec((1, length), lambda i: (0, 0)),
        ],
        out_specs=pl.BlockSpec((rows, columns), lambda i: (i, 0)),
        scratch_shapes=[
            pltpu.VMEM((rows, columns), BF),
            pltpu.VMEM((2 * length, 128), BF),
            pltpu.VMEM((2 * length, 256), BF),
        ],
        compiler_params=pltpu.CompilerParams(vmem_limit_bytes=32 << 20),
        cost_estimate=pl.CostEstimate(
            flops=2 * length * width * w.shape[1] + 4 * length * 640 * columns * 2,
            bytes_accessed=2 * (length * width + width * w.shape[1] + length * columns),
            transcendentals=length * 640 * columns // HEAD,
        ),
        name="attend",
    )(x, w, cosine, sine, docs.reshape(length, 1), docs.reshape(1, length))


def dispatch_kernel(tokens_ref, attn_ref, gain_ref, table_ref, out_ref, resid_ref):
    rows = tokens_ref.shape[0]
    resid = tokens_ref[...].astype(F32) + attn_ref[...].astype(F32)
    resid_ref[...] = resid
    moe_in = rms_norm(resid, gain_ref[...]).astype(BF)
    tail = jnp.concatenate([moe_in[:, MAIN:], jnp.zeros((rows, STEP - TAIL), BF)], axis=1)
    top = table_ref[:, :rows]
    for j in range(3):
        cols = slice(j * STEP, (j + 1) * STEP)
        table = jnp.concatenate([top, table_ref[:, (j + 1) * rows : (j + 2) * rows]], axis=1)
        source = jnp.concatenate([moe_in[:, cols], tail], axis=0)
        out_ref[:, cols] = jnp.dot(table, source, preferred_element_type=F32).astype(BF)
    out_ref[:, 3 * STEP :] = jnp.dot(
        top, moe_in[:, 3 * STEP : MAIN], preferred_element_type=F32
    ).astype(BF)


def dispatch(tokens, attn_out, gain, table):
    rows, width = tokens.shape
    return pl.pallas_call(
        dispatch_kernel,
        out_shape=(
            jax.ShapeDtypeStruct((table.shape[0], MAIN), BF),
            jax.ShapeDtypeStruct((rows, width), F32),
        ),
        in_specs=[VMEM] * 4,
        out_specs=(VMEM, VMEM),
        compiler_params=pltpu.CompilerParams(vmem_limit_bytes=32 << 20),
        cost_estimate=pl.CostEstimate(
            flops=2 * table.shape[0] * 256 * MAIN,
            bytes_accessed=2 * table.shape[0] * (MAIN + 512) + 8 * rows * width,
            transcendentals=0,
        ),
        name="dispatch",
    )(tokens, attn_out, gain.reshape(1, width), table)


def expert_kernel(
    recv_ref, gate_up_ref, down_ref, pick_ref, put_ref, out_ref,
    x_buf, gate_up_buf, down_buf, both_buf, act_buf, y_buf, sems,
):
    total = x_buf.shape[0]
    tiles = [(s, min(512, WIDTH - s)) for s in range(0, WIDTH, 512)]
    copies = []
    for i, (start, size) in enumerate(tiles):
        cols = pl.ds(start, size)
        copies.append(
            pltpu.make_async_copy(gate_up_ref.at[:, cols], gate_up_buf.at[:, cols], sems.at[i])
        )
    down_copy = pltpu.make_async_copy(down_ref, down_buf, sems.at[len(tiles)])
    for copy in copies:
        copy.start()
    down_copy.start()

    blocks = recv_ref.shape[0] // 128
    packed = 128 // SLOTS * CAP

    def unpack(block, carry):
        source = pl.ds(pl.multiple_of(block * 128, 128), 128)
        target = pl.ds(pl.multiple_of(block * packed, packed), packed)
        tail = jnp.zeros((packed, STEP), F32)
        for j in range(3):
            cols = slice(j * STEP, (j + 1) * STEP)
            pair = jnp.dot(pick_ref[j], recv_ref[source, cols], preferred_element_type=F32)
            x_buf[target, cols] = pair[:packed].astype(BF)
            tail = tail + pair[packed:]
        x_buf[target, 3 * STEP : MAIN] = jnp.dot(
            pick_ref[0, :packed], recv_ref[source, 3 * STEP : MAIN], preferred_element_type=F32
        ).astype(BF)
        x_buf[target, MAIN:] = tail[:, :TAIL].astype(BF)
        return carry

    lax.fori_loop(0, blocks, unpack, 0)

    chunk = total // 3
    for i, (start, size) in enumerate(tiles):
        copies[i].wait()

        def multiply(m, carry, start=start, size=size):
            rows = pl.ds(pl.multiple_of(m * chunk, chunk), chunk)
            both_buf[rows, start : start + size] = jnp.dot(
                x_buf[rows, :], gate_up_buf[:, start : start + size], preferred_element_type=F32
            )
            return carry

        lax.fori_loop(0, 3, multiply, 0)

    def activate(m, carry):
        rows = pl.ds(pl.multiple_of(m * 64, 64), 64)
        gate = both_buf[rows, :FF]
        up = both_buf[rows, FF:]
        act_buf[rows, :] = (gate * jax.nn.sigmoid(1.702 * gate) * (up + 1.0)).astype(BF)
        return carry

    lax.fori_loop(0, total // 64, activate, 0)

    down_copy.wait()
    for start, size in tiles:

        def multiply_down(m, carry, start=start, size=size):
            rows = pl.ds(pl.multiple_of(m * chunk, chunk), chunk)
            y_buf[rows, start : start + size] = jnp.dot(
                act_buf[rows, :], down_buf[:, start : start + size], preferred_element_type=F32
            ).astype(BF)
            return carry

        lax.fori_loop(0, 3, multiply_down, 0)

    def pack(block, carry):
        target = pl.ds(pl.multiple_of(block * 128, 128), 128)
        source = pl.ds(pl.multiple_of(block * packed, packed), packed)
        tail = jnp.concatenate(
            [y_buf[source, MAIN:], jnp.zeros((packed, STEP - TAIL), BF)], axis=1
        )
        for j in range(3):
            cols = slice(j * STEP, (j + 1) * STEP)
            pair = jnp.concatenate([y_buf[source, cols], tail], axis=0)
            out_ref[target, cols] = jnp.dot(
                put_ref[j], pair, preferred_element_type=F32
            ).astype(BF)
        out_ref[target, 3 * STEP :] = jnp.dot(
            put_ref[0, :, :packed], y_buf[source, 3 * STEP : MAIN], preferred_element_type=F32
        ).astype(BF)
        return carry

    lax.fori_loop(0, blocks, pack, 0)


def experts(recv, gate_up, down):
    packed = 128 // SLOTS * CAP
    row = jnp.arange(packed, dtype=jnp.int32)
    source, slot = row // CAP, row % CAP
    col = jnp.arange(128, dtype=jnp.int32)[None, :]
    main = (col == (source * SLOTS + slot)[:, None]).astype(BF)
    place = (source * SLOTS + CAP + slot // 3)[:, None]
    pick = jnp.stack(
        [
            jnp.concatenate([main, ((col == place) & (slot % 3 == j)[:, None]).astype(BF)], axis=0)
            for j in range(3)
        ]
    )
    put = pick.transpose(0, 2, 1)
    total = recv.shape[0] // SLOTS * CAP
    return pl.pallas_call(
        expert_kernel,
        out_shape=jax.ShapeDtypeStruct(recv.shape, BF),
        in_specs=[VMEM, ANY, ANY, VMEM, VMEM],
        out_specs=VMEM,
        scratch_shapes=[
            pltpu.VMEM((total, WIDTH), BF),
            pltpu.VMEM((WIDTH, 2 * FF), BF),
            pltpu.VMEM((FF, WIDTH), BF),
            pltpu.VMEM((total, 2 * FF), F32),
            pltpu.VMEM((total, FF), BF),
            pltpu.VMEM((total, WIDTH), BF),
            pltpu.SemaphoreType.DMA((7,)),
        ],
        compiler_params=pltpu.CompilerParams(vmem_limit_bytes=60 << 20),
        cost_estimate=pl.CostEstimate(
            flops=6 * total * FF * WIDTH,
            bytes_accessed=6 * FF * WIDTH + 4 * recv.shape[0] * MAIN,
            transcendentals=total * FF,
        ),
        name="experts",
    )(recv, gate_up, down, pick, put)


def combine_kernel(back_ref, resid_ref, coef_ref, out_ref):
    rows = resid_ref.shape[0]
    wide = 2 * rows
    main = lax.dot_general(coef_ref[:, :wide], back_ref[...], TN, preferred_element_type=F32)
    out_ref[:, :MAIN] = (resid_ref[:, :MAIN] + (main[:rows] + main[rows:])).astype(BF)
    tail = jnp.zeros((rows, STEP), F32)
    for j in range(3):
        part = lax.dot_general(
            coef_ref[:, (j + 1) * wide : (j + 2) * wide],
            back_ref[:, j * STEP : (j + 1) * STEP],
            TN,
            preferred_element_type=F32,
        )
        tail = tail + (part[:rows] + part[rows:])
    out_ref[:, MAIN:] = (resid_ref[:, MAIN:] + tail[:, :TAIL]).astype(BF)


def combine(back, resid, coef):
    rows, width = resid.shape
    return pl.pallas_call(
        combine_kernel,
        out_shape=jax.ShapeDtypeStruct((rows, width), BF),
        in_specs=[VMEM] * 3,
        out_specs=VMEM,
        compiler_params=pltpu.CompilerParams(vmem_limit_bytes=32 << 20),
        cost_estimate=pl.CostEstimate(
            flops=4 * back.shape[0] * rows * (MAIN + 3 * STEP),
            bytes_accessed=2 * back.shape[0] * (MAIN + 1024) + 6 * rows * width,
            transcendentals=0,
        ),
        name="combine",
    )(back, resid, coef)


def routing(expert_ids, gate_weights, experts_count):
    rows = expert_ids.shape[0]
    names = jnp.arange(experts_count, dtype=jnp.int32)
    named = expert_ids.T[:, None, :] == names[None, :, None]
    hit = jnp.any(named, axis=0)
    share = gate_weights / jnp.sum(gate_weights, axis=-1, keepdims=True)
    weight = jnp.sum(jnp.where(named, share.T[:, None, :], 0.0), axis=0)
    index = jnp.arange(rows, dtype=jnp.int32)
    earlier = (index[:, None] < index[None, :]).astype(BF)
    rank = jnp.dot(hit.astype(BF), earlier, preferred_element_type=F32).astype(jnp.int32)
    rank = jnp.where(hit, rank, -1)[:, None, :]
    slot = jnp.arange(SLOTS, dtype=jnp.int32)[None, :, None]
    layers = [(rank == slot) & (slot < CAP)]
    for j in range(3):
        layers.append(
            ((slot == CAP) & (rank == j)) | ((slot == CAP + 1) & (rank == j + 3))
        )
    flat = [layer.reshape(experts_count * SLOTS, rows) for layer in layers]
    table = jnp.concatenate([layer.astype(BF) for layer in flat], axis=1)
    spread = jnp.broadcast_to(
        weight[:, None, :], (experts_count, SLOTS, rows)
    ).reshape(experts_count * SLOTS, rows)
    high = spread.astype(BF)
    low = (spread - high.astype(F32)).astype(BF)
    none = jnp.zeros((), BF)
    coef = jnp.concatenate(
        [jnp.where(layer, part, none) for layer in flat for part in (high, low)], axis=1
    )
    return table, coef


def body(
    tokens,
    positions,
    doc_ids,
    w_query,
    key_weight,
    value_weight,
    w_out,
    attn_gain,
    moe_gain,
    expert_ids,
    gate_weights,
    w_gate_up,
    w_down,
):
    normed = rms_norm(tokens.astype(F32), attn_gain).astype(BF)
    joined = jnp.concatenate([w_query, key_weight, value_weight], axis=1)
    full_joined = lax.all_gather(joined, "dp", axis=0, tiled=False).reshape(-1, joined.shape[1])
    window = lax.all_gather(normed, "tensor", axis=0, tiled=True)
    full_out = lax.all_gather(w_out, "dp", axis=1, tiled=True)

    half = HEAD // 2
    freq = jnp.exp(jnp.arange(half, dtype=F32) * (-2.0 * math.log(150000.0) / HEAD))
    angle = positions[0].astype(F32)[:, None] * freq[None, :]
    cosine, sine = jnp.cos(angle), jnp.sin(angle)
    cosine = jnp.concatenate([cosine] * 4, axis=1)
    sine = jnp.concatenate([-sine, sine] * 2, axis=1)
    experts_count = lax.axis_size("dp") * lax.axis_size("tensor")
    table, coef = routing(expert_ids, gate_weights, experts_count)

    heads = attend(window, full_joined, cosine, sine, doc_ids[0])
    partial_sums = jnp.dot(heads, full_out, preferred_element_type=F32).astype(BF)
    attn_out = lax.psum_scatter(partial_sums, "tensor", scatter_dimension=0, tiled=True)
    outgoing, resid = dispatch(tokens, attn_out, moe_gain, table)
    received = lax.all_to_all(outgoing, ("dp", "tensor"), split_axis=0, concat_axis=0, tiled=True)
    finished = experts(received, w_gate_up[0], w_down[0])
    returned = lax.all_to_all(finished, ("dp", "tensor"), split_axis=0, concat_axis=0, tiled=True)
    return combine(returned, resid, coef)


def solution(mesh):
    placed = (
        P(("dp", "tensor"), None),
        P("dp", None),
        P("dp", None),
        P("dp", "tensor"),
        P("dp", "tensor"),
        P("dp", "tensor"),
        P("tensor", "dp"),
        P(),
        P(),
        P(("dp", "tensor"), None),
        P(("dp", "tensor"), None),
        P(("dp", "tensor"), None, None),
        P(("dp", "tensor"), None, None),
    )
    return jax.shard_map(
        body, mesh=mesh, in_specs=placed, out_specs=P(("dp", "tensor"), None), check_vma=False
    )
```

```python
import math

import jax
import jax.numpy as jnp
from jax import lax
from jax.experimental import pallas as pl
from jax.experimental.pallas import tpu as pltpu
from jax.sharding import PartitionSpec as P

HEAD = 64
WIDTH = 2880
FF = 1440
CAP = 6
SLOTS = 8
MAIN = 2304
TAIL = WIDTH - MAIN
STEP = 640
BF = jnp.bfloat16
F32 = jnp.float32
NT = (((1,), (1,)), ((), ()))
TN = (((0,), (0,)), ((), ()))
VMEM = pl.BlockSpec(memory_space=pltpu.VMEM)
ANY = pl.BlockSpec(memory_space=pl.ANY)


def rms_norm(value_rows, gain):
    mean_square = jnp.mean(value_rows * value_rows, axis=-1, keepdims=True)
    return value_rows * lax.rsqrt(mean_square + 1e-05) * gain


def attend_kernel(
    x_ref, w_ref, cos_ref, sin_ref, docq_ref, dock_ref, out_ref,
    in_buf, out_buf, q_buf, k_buf, v_buf, p_buf, h_buf,
):
    step = pl.program_id(0)
    rows = x_ref.shape[0]
    part = 128
    length = k_buf.shape[0] // 2
    pairs = h_buf.shape[1] // 128
    inner = in_buf.shape[1]
    base = pl.multiple_of(step * rows, rows)
    other_base = pl.multiple_of(length + step * rows, rows)

    @pl.when(step == 0)
    def _():
        shards, depth, _ = w_ref.shape
        for i in range(0, shards, 4):
            four = slice(i * depth, (i + 4) * depth)
            for start in range(0, w_ref.shape[2], 128):
                block = jnp.concatenate(
                    [w_ref[i + j, :, start : start + 128].astype(F32) for j in range(4)], axis=0
                ).astype(BF)
                if start < inner:
                    in_buf[four, start : start + 128] = block
                else:
                    out_buf[four, start - inner : start - inner + 128] = block

    projected = jnp.dot(x_ref[...], in_buf[...], preferred_element_type=F32)
    lanes = lax.broadcasted_iota(jnp.int32, (rows, 128), 1)
    low = (lanes % HEAD) < HEAD // 2
    cosine = cos_ref[...]
    sine = sin_ref[...]

    def turn(pair):
        swapped = jnp.where(
            low, pltpu.roll(pair, 128 - HEAD // 2, 1), pltpu.roll(pair, HEAD // 2, 1)
        )
        return pair * cosine + swapped * sine

    for pair in range(pairs):
        turned = turn(projected[:, pair * 128 : pair * 128 + 128]) * HEAD ** (-0.5)
        for sub in range(rows // part):
            q_buf[sub, pair * part : (pair + 1) * part, :] = turned[
                sub * part : (sub + 1) * part
            ].astype(BF)
    key_value = projected[:, pairs * 128 :]
    turned = turn(key_value)
    first = lanes < HEAD
    crossed = pltpu.roll(key_value, HEAD, 1)
    turned_crossed = pltpu.roll(turned, HEAD, 1)
    one = jnp.where(first, 1.0, 0.0)
    here, there = pl.ds(base, rows), pl.ds(other_base, rows)
    k_buf[here, :] = jnp.where(first, turned, 0.0).astype(BF)
    k_buf[there, :] = jnp.where(first, 0.0, turned_crossed).astype(BF)
    v_buf[here, 0:128] = jnp.where(first, crossed, 0.0).astype(BF)
    v_buf[here, 128:256] = one.astype(BF)
    v_buf[there, 0:128] = jnp.where(first, 0.0, key_value).astype(BF)
    v_buf[there, 128:256] = (1.0 - one).astype(BF)

    def attend(sub, blocks):
        span = blocks * part
        offset = (sub + 1) * part - span
        start = pl.multiple_of(step * rows + offset, part)
        window = pl.ds(start, span)
        other = pl.ds(pl.multiple_of(length + start, part), span)
        docs = dock_ref[:, window]
        row = lax.broadcasted_iota(jnp.int32, (part, span), 0) + (span - part)
        col = lax.broadcasted_iota(jnp.int32, (part, span), 1)
        mine = slice(sub * part, (sub + 1) * part)
        allowed = (row >= col) & (docq_ref[mine, :] == docs)
        query = q_buf[sub]
        both = None
        for i, keys in enumerate((window, other)):
            scores = lax.dot_general(query, k_buf[keys, :], NT, preferred_element_type=F32)
            for pair in range(pairs):
                cut = slice(pair * part, (pair + 1) * part)
                masked = jnp.where(allowed, scores[cut], -1e30)
                largest = jnp.max(masked, axis=-1, keepdims=True)
                p_buf[i, cut, :span] = jnp.exp(masked - largest).astype(BF)
            term = jnp.dot(p_buf[i, :, :span], v_buf[keys, :], preferred_element_type=F32)
            both = term if both is None else both + term
        result = (both[:, :128] / both[:, 128:]).astype(BF)
        for pair in range(pairs):
            h_buf[mine, pair * 128 : (pair + 1) * 128] = result[pair * part : (pair + 1) * part]

    for turns in range(2):

        @pl.when(step == turns)
        def _():
            for sub in range(2):
                attend(sub, turns * 2 + sub + 1)

    @pl.when(step >= 2)
    def _():
        for sub in range(2):
            attend(sub, 5)

    out_ref[...] = lax.dot_general(
        h_buf[...], out_buf[...], NT, preferred_element_type=F32
    ).astype(BF)


def attend(x, w, columns, cosine, sine, docs):
    length, width = x.shape
    inner = columns + 2 * HEAD
    rows = 256
    part = 128
    shards, depth, total = w.shape
    return pl.pallas_call(
        attend_kernel,
        out_shape=jax.ShapeDtypeStruct((length, width), BF),
        grid=(length // rows,),
        in_specs=[
            pl.BlockSpec((rows, width), lambda i: (i, 0)),
            pl.BlockSpec((shards, depth, total), lambda i: (0, 0, 0)),
            pl.BlockSpec((rows, 128), lambda i: (i, 0)),
            pl.BlockSpec((rows, 128), lambda i: (i, 0)),
            pl.BlockSpec((rows, 1), lambda i: (i, 0)),
            pl.BlockSpec((1, length), lambda i: (0, 0)),
        ],
        out_specs=pl.BlockSpec((rows, width), lambda i: (i, 0)),
        scratch_shapes=[
            pltpu.VMEM((width, inner), BF),
            pltpu.VMEM((width, columns), BF),
            pltpu.VMEM((rows // part, columns, 128), BF),
            pltpu.VMEM((2 * length, 128), BF),
            pltpu.VMEM((2 * length, 256), BF),
            pltpu.VMEM((2, columns, 640), BF),
            pltpu.VMEM((rows, columns), BF),
        ],
        compiler_params=pltpu.CompilerParams(vmem_limit_bytes=48 << 20),
        cost_estimate=pl.CostEstimate(
            flops=2 * length * width * total + 4 * length * 640 * columns * 2,
            bytes_accessed=2 * (2 * length * width + width * total),
            transcendentals=length * 640 * columns // HEAD,
        ),
        name="attend",
    )(x, w, cosine, sine, docs.reshape(length, 1), docs.reshape(1, length))


def gather_window(normed):
    size = lax.axis_size("tensor")
    ring = size // 2
    ahead = [(t, (t // 2 + 1) % ring * 2 + t % 2) for t in range(size)]
    back = [(t, (t // 2 + ring - 1) % ring * 2 + t % 2) for t in range(size)]
    across = [(t, t ^ 1) for t in range(size)]
    half = normed.shape[0] // 2
    before = lax.ppermute(normed, "tensor", ahead)
    after = lax.ppermute(normed, "tensor", back)
    far = jnp.concatenate(
        [
            lax.ppermute(before[:half], "tensor", ahead),
            lax.ppermute(after[half:], "tensor", back),
        ],
        axis=0,
    )
    mine = jnp.stack([normed, after, far, before])
    theirs = jnp.stack([lax.ppermute(p, "tensor", across) for p in (normed, after, far, before)])
    index = lax.axis_index("tensor")
    odd = index % 2 == 1
    both = jnp.stack([jnp.where(odd, theirs, mine), jnp.where(odd, mine, theirs)], axis=1)
    return jnp.roll(both, index // 2, axis=0).reshape(-1, normed.shape[1])


def dispatch_kernel(tokens_ref, attn_ref, gain_ref, table_ref, out_ref, resid_ref):
    rows = tokens_ref.shape[0]
    resid = tokens_ref[...].astype(F32) + attn_ref[...].astype(F32)
    resid_ref[...] = resid
    moe_in = rms_norm(resid, gain_ref[...]).astype(BF)
    tail = jnp.concatenate([moe_in[:, MAIN:], jnp.zeros((rows, STEP - TAIL), BF)], axis=1)
    top = table_ref[:, :rows]
    for j in range(3):
        cols = slice(j * STEP, (j + 1) * STEP)
        table = jnp.concatenate([top, table_ref[:, (j + 1) * rows : (j + 2) * rows]], axis=1)
        source = jnp.concatenate([moe_in[:, cols], tail], axis=0)
        out_ref[:, cols] = jnp.dot(table, source, preferred_element_type=F32).astype(BF)
    out_ref[:, 3 * STEP :] = jnp.dot(
        top, moe_in[:, 3 * STEP : MAIN], preferred_element_type=F32
    ).astype(BF)


def dispatch(tokens, attn_out, gain, table):
    rows, width = tokens.shape
    return pl.pallas_call(
        dispatch_kernel,
        out_shape=(
            jax.ShapeDtypeStruct((table.shape[0], MAIN), BF),
            jax.ShapeDtypeStruct((rows, width), F32),
        ),
        in_specs=[VMEM] * 4,
        out_specs=(VMEM, VMEM),
        compiler_params=pltpu.CompilerParams(vmem_limit_bytes=32 << 20),
        cost_estimate=pl.CostEstimate(
            flops=2 * table.shape[0] * 256 * MAIN,
            bytes_accessed=2 * table.shape[0] * (MAIN + 512) + 8 * rows * width,
            transcendentals=0,
        ),
        name="dispatch",
    )(tokens, attn_out, gain.reshape(1, width), table)


def expert_kernel(
    recv_ref, gate_up_ref, down_ref, pick_ref, put_ref, out_ref,
    x_buf, gate_up_buf, down_buf, both_buf, act_buf, y_buf, sems,
):
    total = x_buf.shape[0]
    tiles = [(s, min(512, WIDTH - s)) for s in range(0, WIDTH, 512)]
    copies = []
    for i, (start, size) in enumerate(tiles):
        cols = pl.ds(start, size)
        copies.append(
            pltpu.make_async_copy(gate_up_ref.at[:, cols], gate_up_buf.at[:, cols], sems.at[i])
        )
    down_copy = pltpu.make_async_copy(down_ref, down_buf, sems.at[len(tiles)])
    for copy in copies:
        copy.start()
    down_copy.start()

    blocks = recv_ref.shape[0] // 128
    packed = 128 // SLOTS * CAP

    def unpack(block, carry):
        source = pl.ds(pl.multiple_of(block * 128, 128), 128)
        target = pl.ds(pl.multiple_of(block * packed, packed), packed)
        tail = jnp.zeros((packed, STEP), F32)
        for j in range(3):
            cols = slice(j * STEP, (j + 1) * STEP)
            pair = jnp.dot(pick_ref[j], recv_ref[source, cols], preferred_element_type=F32)
            x_buf[target, cols] = pair[:packed].astype(BF)
            tail = tail + pair[packed:]
        x_buf[target, 3 * STEP : MAIN] = jnp.dot(
            pick_ref[0, :packed], recv_ref[source, 3 * STEP : MAIN], preferred_element_type=F32
        ).astype(BF)
        x_buf[target, MAIN:] = tail[:, :TAIL].astype(BF)
        return carry

    lax.fori_loop(0, blocks, unpack, 0)

    chunk = total // 3
    for i, (start, size) in enumerate(tiles):
        copies[i].wait()

        def multiply(m, carry, start=start, size=size):
            rows = pl.ds(pl.multiple_of(m * chunk, chunk), chunk)
            both_buf[rows, start : start + size] = jnp.dot(
                x_buf[rows, :], gate_up_buf[:, start : start + size], preferred_element_type=F32
            )
            return carry

        lax.fori_loop(0, 3, multiply, 0)

    def activate(m, carry):
        rows = pl.ds(pl.multiple_of(m * 64, 64), 64)
        gate = both_buf[rows, :FF]
        up = both_buf[rows, FF:]
        act_buf[rows, :] = (gate * jax.nn.sigmoid(1.702 * gate) * (up + 1.0)).astype(BF)
        return carry

    lax.fori_loop(0, total // 64, activate, 0)

    down_copy.wait()
    for start, size in tiles:

        def multiply_down(m, carry, start=start, size=size):
            rows = pl.ds(pl.multiple_of(m * chunk, chunk), chunk)
            y_buf[rows, start : start + size] = jnp.dot(
                act_buf[rows, :], down_buf[:, start : start + size], preferred_element_type=F32
            ).astype(BF)
            return carry

        lax.fori_loop(0, 3, multiply_down, 0)

    def pack(block, carry):
        target = pl.ds(pl.multiple_of(block * 128, 128), 128)
        source = pl.ds(pl.multiple_of(block * packed, packed), packed)
        tail = jnp.concatenate(
            [y_buf[source, MAIN:], jnp.zeros((packed, STEP - TAIL), BF)], axis=1
        )
        for j in range(3):
            cols = slice(j * STEP, (j + 1) * STEP)
            pair = jnp.concatenate([y_buf[source, cols], tail], axis=0)
            out_ref[target, cols] = jnp.dot(
                put_ref[j], pair, preferred_element_type=F32
            ).astype(BF)
        out_ref[target, 3 * STEP :] = jnp.dot(
            put_ref[0, :, :packed], y_buf[source, 3 * STEP : MAIN], preferred_element_type=F32
        ).astype(BF)
        return carry

    lax.fori_loop(0, blocks, pack, 0)


def experts(recv, gate_up, down):
    packed = 128 // SLOTS * CAP
    row = jnp.arange(packed, dtype=jnp.int32)
    source, slot = row // CAP, row % CAP
    col = jnp.arange(128, dtype=jnp.int32)[None, :]
    main = (col == (source * SLOTS + slot)[:, None]).astype(BF)
    place = (source * SLOTS + CAP + slot // 3)[:, None]
    pick = jnp.stack(
        [
            jnp.concatenate([main, ((col == place) & (slot % 3 == j)[:, None]).astype(BF)], axis=0)
            for j in range(3)
        ]
    )
    put = pick.transpose(0, 2, 1)
    total = recv.shape[0] // SLOTS * CAP
    return pl.pallas_call(
        expert_kernel,
        out_shape=jax.ShapeDtypeStruct(recv.shape, BF),
        in_specs=[VMEM, ANY, ANY, VMEM, VMEM],
        out_specs=VMEM,
        scratch_shapes=[
            pltpu.VMEM((total, WIDTH), BF),
            pltpu.VMEM((WIDTH, 2 * FF), BF),
            pltpu.VMEM((FF, WIDTH), BF),
            pltpu.VMEM((total, 2 * FF), F32),
            pltpu.VMEM((total, FF), BF),
            pltpu.VMEM((total, WIDTH), BF),
            pltpu.SemaphoreType.DMA((7,)),
        ],
        compiler_params=pltpu.CompilerParams(vmem_limit_bytes=60 << 20),
        cost_estimate=pl.CostEstimate(
            flops=6 * total * FF * WIDTH,
            bytes_accessed=6 * FF * WIDTH + 4 * recv.shape[0] * MAIN,
            transcendentals=total * FF,
        ),
        name="experts",
    )(recv, gate_up, down, pick, put)


def combine_kernel(back_ref, resid_ref, coef_ref, out_ref):
    rows = resid_ref.shape[0]
    wide = 2 * rows
    main = lax.dot_general(coef_ref[:, :wide], back_ref[...], TN, preferred_element_type=F32)
    out_ref[:, :MAIN] = (resid_ref[:, :MAIN] + (main[:rows] + main[rows:])).astype(BF)
    tail = jnp.zeros((rows, STEP), F32)
    for j in range(3):
        part = lax.dot_general(
            coef_ref[:, (j + 1) * wide : (j + 2) * wide],
            back_ref[:, j * STEP : (j + 1) * STEP],
            TN,
            preferred_element_type=F32,
        )
        tail = tail + (part[:rows] + part[rows:])
    out_ref[:, MAIN:] = (resid_ref[:, MAIN:] + tail[:, :TAIL]).astype(BF)


def combine(back, resid, coef):
    rows, width = resid.shape
    return pl.pallas_call(
        combine_kernel,
        out_shape=jax.ShapeDtypeStruct((rows, width), BF),
        in_specs=[VMEM] * 3,
        out_specs=VMEM,
        compiler_params=pltpu.CompilerParams(vmem_limit_bytes=32 << 20),
        cost_estimate=pl.CostEstimate(
            flops=4 * back.shape[0] * rows * (MAIN + 3 * STEP),
            bytes_accessed=2 * back.shape[0] * (MAIN + 1024) + 6 * rows * width,
            transcendentals=0,
        ),
        name="combine",
    )(back, resid, coef)


def routing(expert_ids, gate_weights, experts_count):
    rows = expert_ids.shape[0]
    names = jnp.arange(experts_count, dtype=jnp.int32)
    named = expert_ids.T[:, None, :] == names[None, :, None]
    hit = jnp.any(named, axis=0)
    share = gate_weights / jnp.sum(gate_weights, axis=-1, keepdims=True)
    weight = jnp.sum(jnp.where(named, share.T[:, None, :], 0.0), axis=0)
    index = jnp.arange(rows, dtype=jnp.int32)
    earlier = (index[:, None] < index[None, :]).astype(BF)
    rank = jnp.dot(hit.astype(BF), earlier, preferred_element_type=F32).astype(jnp.int32)
    rank = jnp.where(hit, rank, -1)[:, None, :]
    slot = jnp.arange(SLOTS, dtype=jnp.int32)[None, :, None]
    layers = [(rank == slot) & (slot < CAP)]
    for j in range(3):
        layers.append(
            ((slot == CAP) & (rank == j)) | ((slot == CAP + 1) & (rank == j + 3))
        )
    flat = [layer.reshape(experts_count * SLOTS, rows) for layer in layers]
    table = jnp.concatenate([layer.astype(BF) for layer in flat], axis=1)
    spread = jnp.broadcast_to(
        weight[:, None, :], (experts_count, SLOTS, rows)
    ).reshape(experts_count * SLOTS, rows)
    high = spread.astype(BF)
    low = (spread - high.astype(F32)).astype(BF)
    none = jnp.zeros((), BF)
    coef = jnp.concatenate(
        [jnp.where(layer, part, none) for layer in flat for part in (high, low)], axis=1
    )
    return table, coef


def body(
    tokens,
    positions,
    doc_ids,
    w_query,
    key_weight,
    value_weight,
    w_out,
    attn_gain,
    moe_gain,
    expert_ids,
    gate_weights,
    w_gate_up,
    w_down,
):
    normed = rms_norm(tokens.astype(F32), attn_gain).astype(BF)
    joined = jnp.concatenate([w_query, key_weight, value_weight, w_out.T], axis=1)
    weights = lax.all_gather(joined, "dp", axis=0, tiled=False)
    window = gather_window(normed)

    half = HEAD // 2
    freq = jnp.exp(jnp.arange(half, dtype=F32) * (-2.0 * math.log(150000.0) / HEAD))
    angle = positions[0].astype(F32)[:, None] * freq[None, :]
    cosine, sine = jnp.cos(angle), jnp.sin(angle)
    cosine = jnp.concatenate([cosine] * 4, axis=1)
    sine = jnp.concatenate([-sine, sine] * 2, axis=1)
    experts_count = lax.axis_size("dp") * lax.axis_size("tensor")
    table, coef = routing(expert_ids, gate_weights, experts_count)

    partial_sums = attend(window, weights, w_query.shape[1], cosine, sine, doc_ids[0])
    attn_out = lax.psum_scatter(partial_sums, "tensor", scatter_dimension=0, tiled=True)
    outgoing, resid = dispatch(tokens, attn_out, moe_gain, table)
    received = lax.all_to_all(outgoing, ("dp", "tensor"), split_axis=0, concat_axis=0, tiled=True)
    finished = experts(received, w_gate_up[0], w_down[0])
    returned = lax.all_to_all(finished, ("dp", "tensor"), split_axis=0, concat_axis=0, tiled=True)
    return combine(returned, resid, coef)


def solution(mesh):
    placed = (
        P(("dp", "tensor"), None),
        P("dp", None),
        P("dp", None),
        P("dp", "tensor"),
        P("dp", "tensor"),
        P("dp", "tensor"),
        P("tensor", "dp"),
        P(),
        P(),
        P(("dp", "tensor"), None),
        P(("dp", "tensor"), None),
        P(("dp", "tensor"), None, None),
        P(("dp", "tensor"), None, None),
    )
    return jax.shard_map(
        body, mesh=mesh, in_specs=placed, out_specs=P(("dp", "tensor"), None), check_vma=False
    )
```

```python
import math

import jax
import jax.numpy as jnp
from jax import lax
from jax.experimental import pallas as pl
from jax.experimental.pallas import tpu as pltpu
from jax.sharding import PartitionSpec as P

HEAD = 64
WIDTH = 2880
FF = 1440
CAP = 6
HALF = 3
SLOTS = 8
WIDE = 1152
LEFT = 640
RIGHT = WIDE - LEFT
MAIN = 2 * WIDE
TAIL = WIDTH - MAIN
BF = jnp.bfloat16
F32 = jnp.float32
NT = (((1,), (1,)), ((), ()))
TN = (((0,), (0,)), ((), ()))
VMEM = pl.BlockSpec(memory_space=pltpu.VMEM)
ANY = pl.BlockSpec(memory_space=pl.ANY)


def rms_norm(value_rows, gain):
    mean_square = jnp.mean(value_rows * value_rows, axis=-1, keepdims=True)
    return value_rows * lax.rsqrt(mean_square + 1e-05) * gain


def attend_kernel(
    x_ref, w_ref, cos_ref, sin_ref, docq_ref, dock_ref, out_ref,
    in_buf, out_buf, q_buf, k_buf, v_buf, p_buf, h_buf,
):
    step = pl.program_id(0)
    rows = x_ref.shape[0]
    part = 128
    length = k_buf.shape[0] // 2
    pairs = h_buf.shape[1] // 128
    inner = in_buf.shape[1]
    base = pl.multiple_of(step * rows, rows)
    other_base = pl.multiple_of(length + step * rows, rows)

    @pl.when(step == 0)
    def _():
        shards, depth, _ = w_ref.shape
        for i in range(0, shards, 4):
            four = slice(i * depth, (i + 4) * depth)
            for start in range(0, w_ref.shape[2], 128):
                block = jnp.concatenate(
                    [w_ref[i + j, :, start : start + 128].astype(F32) for j in range(4)], axis=0
                ).astype(BF)
                if start < inner:
                    in_buf[four, start : start + 128] = block
                else:
                    out_buf[four, start - inner : start - inner + 128] = block

    projected = jnp.dot(x_ref[...], in_buf[...], preferred_element_type=F32)
    lanes = lax.broadcasted_iota(jnp.int32, (rows, 128), 1)
    low = (lanes % HEAD) < HEAD // 2
    cosine = cos_ref[...]
    sine = sin_ref[...]

    def turn(pair):
        swapped = jnp.where(
            low, pltpu.roll(pair, 128 - HEAD // 2, 1), pltpu.roll(pair, HEAD // 2, 1)
        )
        return pair * cosine + swapped * sine

    for pair in range(pairs):
        turned = turn(projected[:, pair * 128 : pair * 128 + 128]) * HEAD ** (-0.5)
        for sub in range(rows // part):
            q_buf[sub, pair * part : (pair + 1) * part, :] = turned[
                sub * part : (sub + 1) * part
            ].astype(BF)
    key_value = projected[:, pairs * 128 :]
    turned = turn(key_value)
    first = lanes < HEAD
    crossed = pltpu.roll(key_value, HEAD, 1)
    turned_crossed = pltpu.roll(turned, HEAD, 1)
    one = jnp.where(first, 1.0, 0.0)
    here, there = pl.ds(base, rows), pl.ds(other_base, rows)
    k_buf[here, :] = jnp.where(first, turned, 0.0).astype(BF)
    k_buf[there, :] = jnp.where(first, 0.0, turned_crossed).astype(BF)
    v_buf[here, 0:128] = jnp.where(first, crossed, 0.0).astype(BF)
    v_buf[here, 128:256] = one.astype(BF)
    v_buf[there, 0:128] = jnp.where(first, 0.0, key_value).astype(BF)
    v_buf[there, 128:256] = (1.0 - one).astype(BF)

    def attend(sub, blocks):
        span = blocks * part
        offset = (sub + 1) * part - span
        start = pl.multiple_of(step * rows + offset, part)
        window = pl.ds(start, span)
        other = pl.ds(pl.multiple_of(length + start, part), span)
        docs = dock_ref[:, window]
        row = lax.broadcasted_iota(jnp.int32, (part, span), 0) + (span - part)
        col = lax.broadcasted_iota(jnp.int32, (part, span), 1)
        mine = slice(sub * part, (sub + 1) * part)
        allowed = (row >= col) & (docq_ref[mine, :] == docs)
        query = q_buf[sub]
        both = None
        for i, keys in enumerate((window, other)):
            scores = lax.dot_general(query, k_buf[keys, :], NT, preferred_element_type=F32)
            for pair in range(pairs):
                cut = slice(pair * part, (pair + 1) * part)
                masked = jnp.where(allowed, scores[cut], -1e30)
                largest = jnp.max(masked, axis=-1, keepdims=True)
                p_buf[i, cut, :span] = jnp.exp(masked - largest).astype(BF)
            term = jnp.dot(p_buf[i, :, :span], v_buf[keys, :], preferred_element_type=F32)
            both = term if both is None else both + term
        result = (both[:, :128] / both[:, 128:]).astype(BF)
        for pair in range(pairs):
            h_buf[mine, pair * 128 : (pair + 1) * 128] = result[pair * part : (pair + 1) * part]

    for turns in range(2):

        @pl.when(step == turns)
        def _():
            for sub in range(2):
                attend(sub, turns * 2 + sub + 1)

    @pl.when(step >= 2)
    def _():
        for sub in range(2):
            attend(sub, 5)

    out_ref[...] = lax.dot_general(
        h_buf[...], out_buf[...], NT, preferred_element_type=F32
    ).astype(BF)


def attend(x, w, columns, cosine, sine, docs):
    length, width = x.shape
    inner = columns + 2 * HEAD
    rows = 256
    part = 128
    shards, depth, total = w.shape
    return pl.pallas_call(
        attend_kernel,
        out_shape=jax.ShapeDtypeStruct((length, width), BF),
        grid=(length // rows,),
        in_specs=[
            pl.BlockSpec((rows, width), lambda i: (i, 0)),
            pl.BlockSpec((shards, depth, total), lambda i: (0, 0, 0)),
            pl.BlockSpec((rows, 128), lambda i: (i, 0)),
            pl.BlockSpec((rows, 128), lambda i: (i, 0)),
            pl.BlockSpec((rows, 1), lambda i: (i, 0)),
            pl.BlockSpec((1, length), lambda i: (0, 0)),
        ],
        out_specs=pl.BlockSpec((rows, width), lambda i: (i, 0)),
        scratch_shapes=[
            pltpu.VMEM((width, inner), BF),
            pltpu.VMEM((width, columns), BF),
            pltpu.VMEM((rows // part, columns, 128), BF),
            pltpu.VMEM((2 * length, 128), BF),
            pltpu.VMEM((2 * length, 256), BF),
            pltpu.VMEM((2, columns, 640), BF),
            pltpu.VMEM((rows, columns), BF),
        ],
        compiler_params=pltpu.CompilerParams(vmem_limit_bytes=48 << 20),
        cost_estimate=pl.CostEstimate(
            flops=2 * length * width * total + 4 * length * 640 * columns * 2,
            bytes_accessed=2 * (2 * length * width + width * total),
            transcendentals=length * 640 * columns // HEAD,
        ),
        name="attend",
    )(x, w, cosine, sine, docs.reshape(length, 1), docs.reshape(1, length))


def gather_window(normed):
    size = lax.axis_size("tensor")
    ring = size // 2
    ahead = [(t, (t // 2 + 1) % ring * 2 + t % 2) for t in range(size)]
    back = [(t, (t // 2 + ring - 1) % ring * 2 + t % 2) for t in range(size)]
    across = [(t, t ^ 1) for t in range(size)]
    half = normed.shape[0] // 2
    before = lax.ppermute(normed, "tensor", ahead)
    after = lax.ppermute(normed, "tensor", back)
    far = jnp.concatenate(
        [
            lax.ppermute(before[:half], "tensor", ahead),
            lax.ppermute(after[half:], "tensor", back),
        ],
        axis=0,
    )
    mine = jnp.stack([normed, after, far, before])
    theirs = jnp.stack([lax.ppermute(p, "tensor", across) for p in (normed, after, far, before)])
    index = lax.axis_index("tensor")
    odd = index % 2 == 1
    both = jnp.stack([jnp.where(odd, theirs, mine), jnp.where(odd, mine, theirs)], axis=1)
    return jnp.roll(both, index // 2, axis=0).reshape(-1, normed.shape[1])


def kinds(slot, rank):
    return (
        (slot == rank) & (rank >= 0) & (rank < HALF),
        (slot == rank + HALF) & (rank >= 0) & (rank < HALF),
        ((slot == 6) & (rank == 0)) | ((slot == 7) & (rank == 2)),
        (slot == 6) & (rank == 1),
        (slot == 7) & (rank == 1),
    )


def pieces(rows, tail):
    count = rows.shape[0]
    none = jnp.zeros((count, LEFT - TAIL), rows.dtype)
    left = jnp.concatenate(
        [rows[:, :LEFT], rows[:, WIDE : WIDE + LEFT], jnp.concatenate([tail, none], axis=1)], axis=0
    )
    rest = jnp.concatenate(
        [tail[:, RIGHT:], jnp.zeros((count, RIGHT - (TAIL - RIGHT)), rows.dtype)], axis=1
    )
    right = jnp.concatenate(
        [rows[:, LEFT:WIDE], rows[:, WIDE + LEFT : MAIN], tail[:, :RIGHT], rest], axis=0
    )
    return left, right


def dispatch_kernel(tokens_ref, attn_ref, gain_ref, table_ref, one_ref, two_ref, resid_ref):
    rows = tokens_ref.shape[0]
    resid = tokens_ref[...].astype(F32) + attn_ref[...].astype(F32)
    resid_ref[...] = resid
    moe_in = rms_norm(resid, gain_ref[...]).astype(BF)
    left, right = pieces(moe_in, moe_in[:, MAIN:])
    for part, out_ref in enumerate((one_ref, two_ref)):
        out_ref[:, :LEFT] = jnp.dot(
            table_ref[part, :, : 3 * rows], left, preferred_element_type=F32
        ).astype(BF)
        table = jnp.concatenate(
            [table_ref[part, :, : 2 * rows], table_ref[part, :, 3 * rows :]], axis=1
        )
        out_ref[:, LEFT:] = jnp.dot(table, right, preferred_element_type=F32).astype(BF)


def dispatch(tokens, attn_out, gain, table):
    rows, width = tokens.shape
    sent = jax.ShapeDtypeStruct((table.shape[1], WIDE), BF)
    return pl.pallas_call(
        dispatch_kernel,
        out_shape=(sent, sent, jax.ShapeDtypeStruct((rows, width), F32)),
        in_specs=[VMEM] * 4,
        out_specs=(VMEM, VMEM, VMEM),
        compiler_params=pltpu.CompilerParams(vmem_limit_bytes=56 << 20),
        cost_estimate=pl.CostEstimate(
            flops=2 * table.shape[1] * 1024 * WIDE,
            bytes_accessed=4 * table.shape[1] * (WIDE + 640) + 8 * rows * width,
            transcendentals=0,
        ),
        name="dispatch",
    )(tokens, attn_out, gain.reshape(1, width), table)


def after_kernel(value_ref, other_ref, out_ref):
    pass


def after(value, other):
    return pl.pallas_call(
        after_kernel,
        out_shape=jax.ShapeDtypeStruct(value.shape, value.dtype),
        in_specs=[ANY, ANY],
        out_specs=ANY,
        input_output_aliases={0: 0},
        name="after",
    )(value, other)


def expert_kernel(
    recv_ref, gate_up_ref, down_ref, pick_ref, put_ref, out_ref,
    x_buf, gate_up_buf, down_buf, both_buf, act_buf, y_buf, sems,
):
    total = x_buf.shape[0]
    tiles = [(s, min(512, WIDTH - s)) for s in range(0, WIDTH, 512)]
    copies = []
    for i, (start, size) in enumerate(tiles):
        cols = pl.ds(start, size)
        copies.append(
            pltpu.make_async_copy(gate_up_ref.at[:, cols], gate_up_buf.at[:, cols], sems.at[i])
        )
    down_copy = pltpu.make_async_copy(down_ref, down_buf, sems.at[len(tiles)])
    for copy in copies:
        copy.start()
    down_copy.start()

    blocks = recv_ref.shape[0] // 128
    few = 128 // SLOTS * HALF

    def unpack(block, carry):
        source = pl.ds(pl.multiple_of(block * 128, 128), 128)
        target = pl.ds(pl.multiple_of(block * few, few), few)
        left = jnp.dot(
            pick_ref[: 3 * few, :], recv_ref[source, :LEFT], preferred_element_type=F32
        ).astype(BF)
        right = jnp.dot(pick_ref[...], recv_ref[source, LEFT:], preferred_element_type=F32)
        first = right[3 * few : 4 * few]
        second = right[4 * few :]
        right = right.astype(BF)
        x_buf[target, :LEFT] = left[:few]
        x_buf[target, LEFT:WIDE] = right[:few]
        x_buf[target, WIDE : WIDE + LEFT] = left[few : 2 * few]
        x_buf[target, WIDE + LEFT : MAIN] = right[few : 2 * few]
        tail = left[2 * few :].astype(F32)
        x_buf[target, MAIN : MAIN + RIGHT] = (tail[:, :RIGHT] + first).astype(BF)
        x_buf[target, MAIN + RIGHT :] = (
            tail[:, RIGHT:TAIL] + second[:, : TAIL - RIGHT]
        ).astype(BF)
        return carry

    lax.fori_loop(0, blocks, unpack, 0)

    for i, (start, size) in enumerate(tiles):
        copies[i].wait()
        both_buf[:, start : start + size] = jnp.dot(
            x_buf[...], gate_up_buf[:, start : start + size], preferred_element_type=F32
        )

    def activate(m, carry):
        rows = pl.ds(pl.multiple_of(m * 64, 64), 64)
        gate = both_buf[rows, :FF]
        up = both_buf[rows, FF:]
        act_buf[rows, :] = (gate * jax.nn.sigmoid(1.702 * gate) * (up + 1.0)).astype(BF)
        return carry

    lax.fori_loop(0, total // 64, activate, 0)

    down_copy.wait()
    for start, size in tiles:
        y_buf[:, start : start + size] = jnp.dot(
            act_buf[...], down_buf[:, start : start + size], preferred_element_type=F32
        ).astype(BF)

    def pack(block, carry):
        target = pl.ds(pl.multiple_of(block * 128, 128), 128)
        source = pl.ds(pl.multiple_of(block * few, few), few)
        left, right = pieces(y_buf[source, :], y_buf[source, MAIN:])
        out_ref[target, :LEFT] = jnp.dot(
            put_ref[:, : 3 * few], left, preferred_element_type=F32
        ).astype(BF)
        put = jnp.concatenate([put_ref[:, : 2 * few], put_ref[:, 3 * few :]], axis=1)
        out_ref[target, LEFT:] = jnp.dot(put, right, preferred_element_type=F32).astype(BF)
        return carry

    lax.fori_loop(0, blocks, pack, 0)


def experts(recv, gate_up, down):
    few = 128 // SLOTS * HALF
    row = jnp.arange(few, dtype=jnp.int32)[:, None]
    source, rank = row // HALF, row % HALF
    col = jnp.arange(128, dtype=jnp.int32)[None, :]
    same = col // SLOTS == source
    pick = jnp.concatenate([(mask & same).astype(BF) for mask in kinds(col % SLOTS, rank)], axis=0)
    put = pick.T
    total = recv.shape[0] // SLOTS * HALF
    return pl.pallas_call(
        expert_kernel,
        out_shape=jax.ShapeDtypeStruct(recv.shape, BF),
        in_specs=[VMEM, ANY, ANY, VMEM, VMEM],
        out_specs=VMEM,
        scratch_shapes=[
            pltpu.VMEM((total, WIDTH), BF),
            pltpu.VMEM((WIDTH, 2 * FF), BF),
            pltpu.VMEM((FF, WIDTH), BF),
            pltpu.VMEM((total, 2 * FF), F32),
            pltpu.VMEM((total, FF), BF),
            pltpu.VMEM((total, WIDTH), BF),
            pltpu.SemaphoreType.DMA((7,)),
        ],
        compiler_params=pltpu.CompilerParams(vmem_limit_bytes=56 << 20),
        cost_estimate=pl.CostEstimate(
            flops=6 * total * FF * WIDTH,
            bytes_accessed=6 * FF * WIDTH + 4 * recv.shape[0] * WIDE,
            transcendentals=total * FF,
        ),
        name="experts",
    )(recv, gate_up, down, pick, put)


def combine_kernel(back_ref, resid_ref, coef_ref, out_ref):
    rows = resid_ref.shape[0]
    pair = 2 * rows

    def both(part, at):
        return part[at : at + rows] + part[at + rows : at + pair]

    main = lax.dot_general(coef_ref[:, : 2 * pair], back_ref[...], TN, preferred_element_type=F32)
    out_ref[:, :WIDE] = (resid_ref[:, :WIDE] + both(main, 0)).astype(out_ref.dtype)
    out_ref[:, WIDE:MAIN] = (resid_ref[:, WIDE:MAIN] + both(main, pair)).astype(out_ref.dtype)
    left = lax.dot_general(
        coef_ref[:, 2 * pair : 3 * pair], back_ref[:, :LEFT], TN, preferred_element_type=F32
    )
    right = lax.dot_general(
        coef_ref[:, 3 * pair :], back_ref[:, LEFT:], TN, preferred_element_type=F32
    )
    tail = both(left, 0)
    out_ref[:, MAIN : MAIN + RIGHT] = (
        resid_ref[:, MAIN : MAIN + RIGHT] + (tail[:, :RIGHT] + both(right, 0))
    ).astype(out_ref.dtype)
    out_ref[:, MAIN + RIGHT :] = (
        resid_ref[:, MAIN + RIGHT :]
        + (tail[:, RIGHT:TAIL] + both(right, pair)[:, : TAIL - RIGHT])
    ).astype(out_ref.dtype)


def combine(back, resid, coef, dtype):
    rows, width = resid.shape
    return pl.pallas_call(
        combine_kernel,
        out_shape=jax.ShapeDtypeStruct((rows, width), dtype),
        in_specs=[VMEM] * 3,
        out_specs=VMEM,
        compiler_params=pltpu.CompilerParams(vmem_limit_bytes=32 << 20),
        cost_estimate=pl.CostEstimate(
            flops=4 * back.shape[0] * rows * (MAIN + 2 * WIDE),
            bytes_accessed=2 * back.shape[0] * (WIDE + 1280) + 8 * rows * width,
            transcendentals=0,
        ),
        name="combine",
    )(back, resid, coef)


def routing(expert_ids, gate_weights, experts_count):
    rows = expert_ids.shape[0]
    names = jnp.arange(experts_count, dtype=jnp.int32)
    named = expert_ids.T[:, None, :] == names[None, :, None]
    hit = jnp.any(named, axis=0)
    share = gate_weights / jnp.sum(gate_weights, axis=-1, keepdims=True)
    weight = jnp.sum(jnp.where(named, share.T[:, None, :], 0.0), axis=0)
    index = jnp.arange(rows, dtype=jnp.int32)
    earlier = (index[:, None] < index[None, :]).astype(BF)
    rank = jnp.dot(hit.astype(BF), earlier, preferred_element_type=F32).astype(jnp.int32)
    rank = jnp.where(hit, rank, -CAP)
    size = experts_count * SLOTS
    spread = jnp.broadcast_to(rank[:, None, :], (experts_count, SLOTS, rows)).reshape(size, rows)
    slot = lax.broadcasted_iota(jnp.int32, (size, rows), 0) % SLOTS
    weight = jnp.broadcast_to(weight[:, None, :], (experts_count, SLOTS, rows)).reshape(size, rows)
    high = weight.astype(BF)
    low = (weight - high.astype(F32)).astype(BF)
    none = jnp.zeros((), BF)
    tables, coefs = [], []
    for part in range(CAP // HALF):
        masks = kinds(slot, spread - part * HALF)
        tables.append(jnp.concatenate([mask.astype(BF) for mask in masks], axis=1))
        coefs.append(
            jnp.concatenate(
                [jnp.where(mask, term, none) for mask in masks for term in (high, low)], axis=1
            )
        )
    return jnp.stack(tables), coefs


def body(
    tokens,
    positions,
    doc_ids,
    w_query,
    key_weight,
    value_weight,
    w_out,
    attn_gain,
    moe_gain,
    expert_ids,
    gate_weights,
    w_gate_up,
    w_down,
):
    normed = rms_norm(tokens.astype(F32), attn_gain).astype(BF)
    joined = jnp.concatenate([w_query, key_weight, value_weight, w_out.T], axis=1)
    weights = lax.all_gather(joined, "dp", axis=0, tiled=False)
    window = gather_window(normed)

    half = HEAD // 2
    freq = jnp.exp(jnp.arange(half, dtype=F32) * (-2.0 * math.log(150000.0) / HEAD))
    angle = positions[0].astype(F32)[:, None] * freq[None, :]
    cosine, sine = jnp.cos(angle), jnp.sin(angle)
    cosine = jnp.concatenate([cosine] * 4, axis=1)
    sine = jnp.concatenate([-sine, sine] * 2, axis=1)
    experts_count = lax.axis_size("dp") * lax.axis_size("tensor")
    table, coef = routing(expert_ids, gate_weights, experts_count)

    partial_sums = attend(window, weights, w_query.shape[1], cosine, sine, doc_ids[0])
    attn_out = lax.psum_scatter(partial_sums, "tensor", scatter_dimension=0, tiled=True)
    first, second, resid = dispatch(tokens, attn_out, moe_gain, table)
    gate_up, down = w_gate_up[0], w_down[0]

    def exchange(blocks):
        return lax.all_to_all(blocks, ("dp", "tensor"), split_axis=0, concat_axis=0, tiled=True)

    first_in = exchange(first)
    second_in = exchange(after(second, first_in))
    first_back = exchange(experts(first_in, gate_up, down))
    second_back = exchange(experts(second_in, gate_up, down))
    mixed = combine(first_back, resid, coef[0], F32)
    return combine(second_back, mixed, coef[1], BF)


def solution(mesh):
    placed = (
        P(("dp", "tensor"), None),
        P("dp", None),
        P("dp", None),
        P("dp", "tensor"),
        P("dp", "tensor"),
        P("dp", "tensor"),
        P("tensor", "dp"),
        P(),
        P(),
        P(("dp", "tensor"), None),
        P(("dp", "tensor"), None),
        P(("dp", "tensor"), None, None),
        P(("dp", "tensor"), None, None),
    )
    return jax.shard_map(
        body, mesh=mesh, in_specs=placed, out_specs=P(("dp", "tensor"), None), check_vma=False
    )
```

```python
import math

import jax
import jax.numpy as jnp
from jax import lax
from jax.experimental import pallas as pl
from jax.experimental.pallas import tpu as pltpu
from jax.sharding import PartitionSpec as P

HEAD = 64
WIDTH = 2880
FF = 1440
CAP = 6
HALF = 3
SLOTS = 8
WIDE = 1152
LEFT = 640
RIGHT = WIDE - LEFT
MAIN = 2 * WIDE
TAIL = WIDTH - MAIN
GATHERED = 768
BF = jnp.bfloat16
F32 = jnp.float32
NT = (((1,), (1,)), ((), ()))
VMEM = pl.BlockSpec(memory_space=pltpu.VMEM)
ANY = pl.BlockSpec(memory_space=pl.ANY)


def rms_norm(value_rows, gain):
    mean_square = jnp.mean(value_rows * value_rows, axis=-1, keepdims=True)
    return value_rows * lax.rsqrt(mean_square + 1e-05) * gain


def attend_kernel(
    x_ref, w_ref, rest_ref, cos_ref, sin_ref, docq_ref, dock_ref, out_ref,
    in_buf, out_buf, q_buf, k_buf, v_buf, p_buf, h_buf,
):
    step = pl.program_id(0)
    rows = x_ref.shape[0]
    part = 128
    length = k_buf.shape[0] // 2
    pairs = h_buf.shape[1] // 128
    inner = in_buf.shape[1]
    base = pl.multiple_of(step * rows, rows)
    other_base = pl.multiple_of(length + step * rows, rows)

    @pl.when(step == 0)
    def _():
        shards, depth, _ = w_ref.shape
        for i in range(0, shards, 4):
            four = slice(i * depth, (i + 4) * depth)
            at = 0
            for ref in (w_ref, rest_ref):
                for start in range(0, ref.shape[2], 128):
                    block = jnp.concatenate(
                        [ref[i + j, :, start : start + 128].astype(F32) for j in range(4)], axis=0
                    ).astype(BF)
                    if at < inner:
                        in_buf[four, at : at + 128] = block
                    else:
                        out_buf[four, at - inner : at - inner + 128] = block
                    at += 128

    projected = jnp.dot(x_ref[...], in_buf[...], preferred_element_type=F32)
    lanes = lax.broadcasted_iota(jnp.int32, (rows, 128), 1)
    low = (lanes % HEAD) < HEAD // 2
    cosine = cos_ref[...]
    sine = sin_ref[...]

    def turn(pair):
        swapped = jnp.where(
            low, pltpu.roll(pair, 128 - HEAD // 2, 1), pltpu.roll(pair, HEAD // 2, 1)
        )
        return pair * cosine + swapped * sine

    for pair in range(pairs):
        turned = turn(projected[:, pair * 128 : pair * 128 + 128]) * HEAD ** (-0.5)
        for sub in range(rows // part):
            q_buf[sub, pair * part : (pair + 1) * part, :] = turned[
                sub * part : (sub + 1) * part
            ].astype(BF)
    key_value = projected[:, pairs * 128 :]
    turned = turn(key_value)
    first = lanes < HEAD
    crossed = pltpu.roll(key_value, HEAD, 1)
    turned_crossed = pltpu.roll(turned, HEAD, 1)
    one = jnp.where(first, 1.0, 0.0)
    here, there = pl.ds(base, rows), pl.ds(other_base, rows)
    k_buf[here, :] = jnp.where(first, turned, 0.0).astype(BF)
    k_buf[there, :] = jnp.where(first, 0.0, turned_crossed).astype(BF)
    v_buf[here, 0:128] = jnp.where(first, crossed, 0.0).astype(BF)
    v_buf[here, 128:256] = one.astype(BF)
    v_buf[there, 0:128] = jnp.where(first, 0.0, key_value).astype(BF)
    v_buf[there, 128:256] = (1.0 - one).astype(BF)

    def attend(sub, blocks):
        span = blocks * part
        offset = (sub + 1) * part - span
        start = pl.multiple_of(step * rows + offset, part)
        window = pl.ds(start, span)
        other = pl.ds(pl.multiple_of(length + start, part), span)
        docs = dock_ref[:, window]
        row = lax.broadcasted_iota(jnp.int32, (part, span), 0) + (span - part)
        col = lax.broadcasted_iota(jnp.int32, (part, span), 1)
        mine = slice(sub * part, (sub + 1) * part)
        allowed = (row >= col) & (docq_ref[mine, :] == docs)
        query = q_buf[sub]
        both = None
        for i, keys in enumerate((window, other)):
            scores = lax.dot_general(query, k_buf[keys, :], NT, preferred_element_type=F32)
            for pair in range(pairs):
                cut = slice(pair * part, (pair + 1) * part)
                masked = jnp.where(allowed, scores[cut], -1e30)
                largest = jnp.max(masked, axis=-1, keepdims=True)
                p_buf[i, cut, :span] = jnp.exp(masked - largest).astype(BF)
            term = jnp.dot(p_buf[i, :, :span], v_buf[keys, :], preferred_element_type=F32)
            both = term if both is None else both + term
        result = (both[:, :128] / both[:, 128:]).astype(BF)
        for pair in range(pairs):
            h_buf[mine, pair * 128 : (pair + 1) * 128] = result[pair * part : (pair + 1) * part]

    for turns in range(2):

        @pl.when(step == turns)
        def _():
            for sub in range(2):
                attend(sub, turns * 2 + sub + 1)

    @pl.when(step >= 2)
    def _():
        for sub in range(2):
            attend(sub, 5)

    out_ref[...] = lax.dot_general(
        h_buf[...], out_buf[...], NT, preferred_element_type=F32
    ).astype(BF)


def attend(x, w, rest, columns, cosine, sine, docs):
    length, width = x.shape
    inner = columns + 2 * HEAD
    rows = 256
    part = 128
    shards, depth, _ = w.shape
    total = inner + columns
    return pl.pallas_call(
        attend_kernel,
        out_shape=jax.ShapeDtypeStruct((length, width), BF),
        grid=(length // rows,),
        in_specs=[
            pl.BlockSpec((rows, width), lambda i: (i, 0)),
            pl.BlockSpec(w.shape, lambda i: (0, 0, 0)),
            pl.BlockSpec(rest.shape, lambda i: (0, 0, 0)),
            pl.BlockSpec((rows, 128), lambda i: (i, 0)),
            pl.BlockSpec((rows, 128), lambda i: (i, 0)),
            pl.BlockSpec((rows, 1), lambda i: (i, 0)),
            pl.BlockSpec((1, length), lambda i: (0, 0)),
        ],
        out_specs=pl.BlockSpec((rows, width), lambda i: (i, 0)),
        scratch_shapes=[
            pltpu.VMEM((width, inner), BF),
            pltpu.VMEM((width, columns), BF),
            pltpu.VMEM((rows // part, columns, 128), BF),
            pltpu.VMEM((2 * length, 128), BF),
            pltpu.VMEM((2 * length, 256), BF),
            pltpu.VMEM((2, columns, 640), BF),
            pltpu.VMEM((rows, columns), BF),
        ],
        compiler_params=pltpu.CompilerParams(vmem_limit_bytes=48 << 20),
        cost_estimate=pl.CostEstimate(
            flops=2 * length * width * total + 4 * length * 640 * columns * 2,
            bytes_accessed=2 * (2 * length * width + width * total),
            transcendentals=length * 640 * columns // HEAD,
        ),
        name="attend",
    )(x, w, rest, cosine, sine, docs.reshape(length, 1), docs.reshape(1, length))


def gather_window(normed):
    size = lax.axis_size("tensor")
    ring = size // 2
    ahead = [(t, (t // 2 + 1) % ring * 2 + t % 2) for t in range(size)]
    back = [(t, (t // 2 + ring - 1) % ring * 2 + t % 2) for t in range(size)]
    across = [(t, t ^ 1) for t in range(size)]
    half = normed.shape[0] // 2
    before = lax.ppermute(normed, "tensor", ahead)
    after = lax.ppermute(normed, "tensor", back)
    far = jnp.concatenate(
        [
            lax.ppermute(before[:half], "tensor", ahead),
            lax.ppermute(after[half:], "tensor", back),
        ],
        axis=0,
    )
    mine = jnp.stack([normed, after, far, before])
    theirs = jnp.stack([lax.ppermute(p, "tensor", across) for p in (normed, after, far, before)])
    index = lax.axis_index("tensor")
    odd = index % 2 == 1
    both = jnp.stack([jnp.where(odd, theirs, mine), jnp.where(odd, mine, theirs)], axis=1)
    return jnp.roll(both, index // 2, axis=0).reshape(-1, normed.shape[1])


def kinds(slot, rank):
    return (
        (slot == rank) & (rank >= 0) & (rank < HALF),
        (slot == rank + HALF) & (rank >= 0) & (rank < HALF),
        ((slot == 6) & (rank == 0)) | ((slot == 7) & (rank == 2)),
        (slot == 6) & (rank == 1),
        (slot == 7) & (rank == 1),
    )


def pieces(rows, tail):
    count = rows.shape[0]
    none = jnp.zeros((count, LEFT - TAIL), rows.dtype)
    left = jnp.concatenate(
        [rows[:, :LEFT], rows[:, WIDE : WIDE + LEFT], jnp.concatenate([tail, none], axis=1)], axis=0
    )
    rest = jnp.concatenate(
        [tail[:, RIGHT:], jnp.zeros((count, RIGHT - (TAIL - RIGHT)), rows.dtype)], axis=1
    )
    right = jnp.concatenate(
        [rows[:, LEFT:WIDE], rows[:, WIDE + LEFT : MAIN], tail[:, :RIGHT], rest], axis=0
    )
    return left, right


def fill(moe_in, table_ref, out_ref):
    rows = moe_in.shape[0]
    left, right = pieces(moe_in, moe_in[:, MAIN:])
    out_ref[:, :LEFT] = jnp.dot(
        table_ref[:, : 3 * rows], left, preferred_element_type=F32
    ).astype(BF)
    table = jnp.concatenate([table_ref[:, : 2 * rows], table_ref[:, 3 * rows :]], axis=1)
    out_ref[:, LEFT:] = jnp.dot(table, right, preferred_element_type=F32).astype(BF)


def dispatch_kernel(tokens_ref, attn_ref, gain_ref, table_ref, out_ref, resid_ref, in_ref):
    resid = tokens_ref[...].astype(F32) + attn_ref[...].astype(F32)
    resid_ref[...] = resid
    moe_in = rms_norm(resid, gain_ref[...]).astype(BF)
    in_ref[...] = moe_in
    fill(moe_in, table_ref, out_ref)


def refill_kernel(in_ref, table_ref, out_ref):
    fill(in_ref[...], table_ref, out_ref)


def dispatch(tokens, attn_out, gain, tables):
    rows, width = tokens.shape
    sent = jax.ShapeDtypeStruct((tables[0].shape[0], WIDE), BF)
    common = dict(
        compiler_params=pltpu.CompilerParams(vmem_limit_bytes=56 << 20),
        cost_estimate=pl.CostEstimate(
            flops=2 * sent.shape[0] * 512 * WIDE,
            bytes_accessed=2 * sent.shape[0] * (WIDE + 640) + 8 * rows * width,
            transcendentals=0,
        ),
    )
    first, resid, moe_in = pl.pallas_call(
        dispatch_kernel,
        out_shape=(
            sent,
            jax.ShapeDtypeStruct((rows, width), F32),
            jax.ShapeDtypeStruct((rows, width), BF),
        ),
        in_specs=[VMEM] * 4,
        out_specs=(VMEM,) * 3,
        name="dispatch",
        **common,
    )(tokens, attn_out, gain.reshape(1, width), tables[0])
    second = pl.pallas_call(
        refill_kernel, out_shape=sent, in_specs=[VMEM] * 2, out_specs=VMEM, name="refill", **common
    )(moe_in, tables[1])
    return first, second, resid


def after_kernel(value_ref, other_ref, out_ref):
    pass


def after(value, other):
    return pl.pallas_call(
        after_kernel,
        out_shape=jax.ShapeDtypeStruct(value.shape, value.dtype),
        in_specs=[ANY, ANY],
        out_specs=ANY,
        input_output_aliases={0: 0},
        name="after",
    )(value, other)


def expert_kernel(
    recv_ref, gate_up_ref, down_ref, pick_ref, put_ref, out_ref,
    x_buf, gate_up_buf, down_buf, both_buf, act_buf, y_buf, sems,
):
    total = x_buf.shape[0]
    tiles = [(s, min(512, WIDTH - s)) for s in range(0, WIDTH, 512)]
    copies = []
    for i, (start, size) in enumerate(tiles):
        cols = pl.ds(start, size)
        copies.append(
            pltpu.make_async_copy(gate_up_ref.at[:, cols], gate_up_buf.at[:, cols], sems.at[i])
        )
    down_copy = pltpu.make_async_copy(down_ref, down_buf, sems.at[len(tiles)])
    for copy in copies:
        copy.start()
    down_copy.start()

    blocks = recv_ref.shape[0] // 128
    few = 128 // SLOTS * HALF

    def unpack(block, carry):
        source = pl.ds(pl.multiple_of(block * 128, 128), 128)
        target = pl.ds(pl.multiple_of(block * few, few), few)
        left = jnp.dot(
            pick_ref[: 3 * few, :], recv_ref[source, :LEFT], preferred_element_type=F32
        ).astype(BF)
        right = jnp.dot(pick_ref[...], recv_ref[source, LEFT:], preferred_element_type=F32)
        first = right[3 * few : 4 * few]
        second = right[4 * few :]
        right = right.astype(BF)
        x_buf[target, :LEFT] = left[:few]
        x_buf[target, LEFT:WIDE] = right[:few]
        x_buf[target, WIDE : WIDE + LEFT] = left[few : 2 * few]
        x_buf[target, WIDE + LEFT : MAIN] = right[few : 2 * few]
        tail = left[2 * few :].astype(F32)
        x_buf[target, MAIN : MAIN + RIGHT] = (tail[:, :RIGHT] + first).astype(BF)
        x_buf[target, MAIN + RIGHT :] = (
            tail[:, RIGHT:TAIL] + second[:, : TAIL - RIGHT]
        ).astype(BF)
        return carry

    lax.fori_loop(0, blocks, unpack, 0)

    for i, (start, size) in enumerate(tiles):
        copies[i].wait()
        both_buf[:, start : start + size] = jnp.dot(
            x_buf[...], gate_up_buf[:, start : start + size], preferred_element_type=F32
        )

    def activate(m, carry):
        rows = pl.ds(pl.multiple_of(m * 64, 64), 64)
        gate = both_buf[rows, :FF]
        up = both_buf[rows, FF:]
        act_buf[rows, :] = (gate * jax.nn.sigmoid(1.702 * gate) * (up + 1.0)).astype(BF)
        return carry

    lax.fori_loop(0, total // 64, activate, 0)

    down_copy.wait()
    for start, size in tiles:
        y_buf[:, start : start + size] = jnp.dot(
            act_buf[...], down_buf[:, start : start + size], preferred_element_type=F32
        ).astype(BF)

    def pack(block, carry):
        target = pl.ds(pl.multiple_of(block * 128, 128), 128)
        source = pl.ds(pl.multiple_of(block * few, few), few)
        left, right = pieces(y_buf[source, :], y_buf[source, MAIN:])
        out_ref[target, :LEFT] = jnp.dot(
            put_ref[:, : 3 * few], left, preferred_element_type=F32
        ).astype(BF)
        put = jnp.concatenate([put_ref[:, : 2 * few], put_ref[:, 3 * few :]], axis=1)
        out_ref[target, LEFT:] = jnp.dot(put, right, preferred_element_type=F32).astype(BF)
        return carry

    lax.fori_loop(0, blocks, pack, 0)


def experts(recv, gate_up, down):
    few = 128 // SLOTS * HALF
    row = jnp.arange(few, dtype=jnp.int32)[:, None]
    source, rank = row // HALF, row % HALF
    col = jnp.arange(128, dtype=jnp.int32)[None, :]
    same = col // SLOTS == source
    pick = jnp.concatenate([(mask & same).astype(BF) for mask in kinds(col % SLOTS, rank)], axis=0)
    put = pick.T
    total = recv.shape[0] // SLOTS * HALF
    return pl.pallas_call(
        expert_kernel,
        out_shape=jax.ShapeDtypeStruct(recv.shape, BF),
        in_specs=[VMEM, ANY, ANY, VMEM, VMEM],
        out_specs=VMEM,
        scratch_shapes=[
            pltpu.VMEM((total, WIDTH), BF),
            pltpu.VMEM((WIDTH, 2 * FF), BF),
            pltpu.VMEM((FF, WIDTH), BF),
            pltpu.VMEM((total, 2 * FF), F32),
            pltpu.VMEM((total, FF), BF),
            pltpu.VMEM((total, WIDTH), BF),
            pltpu.SemaphoreType.DMA((7,)),
        ],
        compiler_params=pltpu.CompilerParams(vmem_limit_bytes=56 << 20),
        cost_estimate=pl.CostEstimate(
            flops=6 * total * FF * WIDTH,
            bytes_accessed=6 * FF * WIDTH + 4 * recv.shape[0] * WIDE,
            transcendentals=total * FF,
        ),
        name="experts",
    )(recv, gate_up, down, pick, put)


def combine_kernel(back_ref, resid_ref, coef_ref, out_ref):
    rows = resid_ref.shape[0]
    pair = 2 * rows

    def both(part, at):
        return part[at : at + rows] + part[at + rows : at + pair]

    main = jnp.dot(coef_ref[: 2 * pair, :], back_ref[...], preferred_element_type=F32)
    out_ref[:, :WIDE] = (resid_ref[:, :WIDE] + both(main, 0)).astype(out_ref.dtype)
    out_ref[:, WIDE:MAIN] = (resid_ref[:, WIDE:MAIN] + both(main, pair)).astype(out_ref.dtype)
    left = jnp.dot(
        coef_ref[2 * pair : 3 * pair, :], back_ref[:, :LEFT], preferred_element_type=F32
    )
    right = jnp.dot(coef_ref[3 * pair :, :], back_ref[:, LEFT:], preferred_element_type=F32)
    tail = both(left, 0)
    out_ref[:, MAIN : MAIN + RIGHT] = (
        resid_ref[:, MAIN : MAIN + RIGHT] + (tail[:, :RIGHT] + both(right, 0))
    ).astype(out_ref.dtype)
    out_ref[:, MAIN + RIGHT :] = (
        resid_ref[:, MAIN + RIGHT :]
        + (tail[:, RIGHT:TAIL] + both(right, pair)[:, : TAIL - RIGHT])
    ).astype(out_ref.dtype)


def combine(back, resid, coef, dtype):
    rows, width = resid.shape
    return pl.pallas_call(
        combine_kernel,
        out_shape=jax.ShapeDtypeStruct((rows, width), dtype),
        in_specs=[VMEM] * 3,
        out_specs=VMEM,
        compiler_params=pltpu.CompilerParams(vmem_limit_bytes=56 << 20),
        cost_estimate=pl.CostEstimate(
            flops=4 * back.shape[0] * rows * (MAIN + 2 * WIDE),
            bytes_accessed=2 * back.shape[0] * (WIDE + 1280) + 8 * rows * width,
            transcendentals=0,
        ),
        name="combine",
    )(back, resid, coef)


def routing(expert_ids, gate_weights, experts_count):
    rows = expert_ids.shape[0]
    names = jnp.arange(experts_count, dtype=jnp.int32)
    named = expert_ids.T[:, None, :] == names[None, :, None]
    hit = jnp.any(named, axis=0)
    share = gate_weights / jnp.sum(gate_weights, axis=-1, keepdims=True)
    weight = jnp.sum(jnp.where(named, share.T[:, None, :], 0.0), axis=0)
    index = jnp.arange(rows, dtype=jnp.int32)
    earlier = (index[:, None] < index[None, :]).astype(BF)
    rank = jnp.dot(hit.astype(BF), earlier, preferred_element_type=F32).astype(jnp.int32)
    rank = jnp.where(hit, rank, -CAP)
    size = experts_count * SLOTS
    spread = jnp.broadcast_to(rank[:, None, :], (experts_count, SLOTS, rows)).reshape(size, rows)
    slot = lax.broadcasted_iota(jnp.int32, (size, rows), 0) % SLOTS
    weight = jnp.broadcast_to(weight[:, None, :], (experts_count, SLOTS, rows)).reshape(size, rows)
    high = weight.astype(BF)
    low = (weight - high.astype(F32)).astype(BF)
    none = jnp.zeros((), BF)
    tables, coefs = [], []
    for part in range(CAP // HALF):
        masks = kinds(slot, spread - part * HALF)
        tables.append(jnp.concatenate([mask.astype(BF) for mask in masks], axis=1))
        coefs.append(
            jnp.concatenate(
                [jnp.where(mask, term, none) for mask in masks for term in (high, low)], axis=1
            ).T
        )
    return tables, coefs


def body(
    tokens,
    positions,
    doc_ids,
    w_query,
    key_weight,
    value_weight,
    w_out,
    attn_gain,
    moe_gain,
    expert_ids,
    gate_weights,
    w_gate_up,
    w_down,
):
    normed = rms_norm(tokens.astype(F32), attn_gain).astype(BF)
    joined = jnp.concatenate([w_query, key_weight, value_weight, w_out.T], axis=1)
    weights = lax.all_gather(joined[:, :GATHERED], "dp", axis=0, tiled=False)
    others = jnp.broadcast_to(
        joined[None, :, GATHERED:],
        (lax.axis_size("dp"), joined.shape[0], joined.shape[1] - GATHERED),
    )
    others = lax.all_to_all(others, "dp", split_axis=0, concat_axis=0, tiled=True)
    window = gather_window(normed)

    half = HEAD // 2
    freq = jnp.exp(jnp.arange(half, dtype=F32) * (-2.0 * math.log(150000.0) / HEAD))
    angle = positions[0].astype(F32)[:, None] * freq[None, :]
    cosine, sine = jnp.cos(angle), jnp.sin(angle)
    cosine = jnp.concatenate([cosine] * 4, axis=1)
    sine = jnp.concatenate([-sine, sine] * 2, axis=1)
    experts_count = lax.axis_size("dp") * lax.axis_size("tensor")
    tables, coef = routing(expert_ids, gate_weights, experts_count)

    partial_sums = attend(window, weights, others, w_query.shape[1], cosine, sine, doc_ids[0])
    attn_out = lax.psum_scatter(partial_sums, "tensor", scatter_dimension=0, tiled=True)
    first, second, resid = dispatch(tokens, attn_out, moe_gain, tables)
    gate_up, down = w_gate_up[0], w_down[0]

    def exchange(blocks):
        return lax.all_to_all(blocks, ("dp", "tensor"), split_axis=0, concat_axis=0, tiled=True)

    first_in = exchange(first)
    second_in = exchange(after(second, first_in))
    first_back = exchange(experts(first_in, gate_up, down))
    second_back = exchange(experts(second_in, gate_up, down))
    mixed = combine(first_back, resid, coef[0], F32)
    return combine(second_back, mixed, coef[1], BF)


def solution(mesh):
    placed = (
        P(("dp", "tensor"), None),
        P("dp", None),
        P("dp", None),
        P("dp", "tensor"),
        P("dp", "tensor"),
        P("dp", "tensor"),
        P("tensor", "dp"),
        P(),
        P(),
        P(("dp", "tensor"), None),
        P(("dp", "tensor"), None),
        P(("dp", "tensor"), None, None),
        P(("dp", "tensor"), None, None),
    )
    return jax.shard_map(
        body, mesh=mesh, in_specs=placed, out_specs=P(("dp", "tensor"), None), check_vma=False
    )
```

```python
import math

import jax
import jax.numpy as jnp
from jax import lax
from jax.experimental import pallas as pl
from jax.experimental.pallas import tpu as pltpu
from jax.sharding import PartitionSpec as P

HEAD = 64
WIDTH = 2880
FF = 1440
CAP = 6
ATTEND_ROWS = 256
SPANS = 5
HALF = 3
SLOTS = 8
WIDE = 1152
LEFT = 640
RIGHT = WIDE - LEFT
MAIN = 2 * WIDE
TAIL = WIDTH - MAIN
BF = jnp.bfloat16
F32 = jnp.float32
NT = (((1,), (1,)), ((), ()))
VMEM = pl.BlockSpec(memory_space=pltpu.VMEM)
ANY = pl.BlockSpec(memory_space=pl.ANY)


def rms_norm(value_rows, gain):
    mean_square = jnp.mean(value_rows * value_rows, axis=-1, keepdims=True)
    return value_rows * lax.rsqrt(mean_square + 1e-05) * gain


def attend_kernel(
    spans_ref, x_ref, w_ref, cos_ref, sin_ref, docq_ref, dock_ref, out_ref,
    in_buf, out_buf, q_buf, k_buf, v_buf, p_buf, h_buf,
):
    step = pl.program_id(0)
    rows = x_ref.shape[0]
    part = 128
    subs = rows // part
    length = k_buf.shape[0] // 2
    pairs = h_buf.shape[1] // 128
    inner = in_buf.shape[1]
    base = pl.multiple_of(step * rows, rows)
    other_base = pl.multiple_of(length + step * rows, rows)

    @pl.when(step == 0)
    def _():
        shards, depth, _ = w_ref.shape
        for i in range(0, shards, 4):
            four = slice(i * depth, (i + 4) * depth)
            for at in range(0, w_ref.shape[2], 128):
                block = jnp.concatenate(
                    [w_ref[i + j, :, at : at + 128].astype(F32) for j in range(4)], axis=0
                ).astype(BF)
                if at < inner:
                    in_buf[four, at : at + 128] = block
                else:
                    out_buf[four, at - inner : at - inner + 128] = block

    projected = jnp.dot(x_ref[...], in_buf[...], preferred_element_type=F32)
    lanes = lax.broadcasted_iota(jnp.int32, (rows, 128), 1)
    low = (lanes % HEAD) < HEAD // 2
    cosine = cos_ref[...]
    sine = sin_ref[...]

    def turn(pair):
        swapped = jnp.where(
            low, pltpu.roll(pair, 128 - HEAD // 2, 1), pltpu.roll(pair, HEAD // 2, 1)
        )
        return pair * cosine + swapped * sine

    for pair in range(pairs):
        turned = turn(projected[:, pair * 128 : pair * 128 + 128]) * HEAD ** (-0.5)
        for sub in range(subs):
            q_buf[sub, pair * part : (pair + 1) * part, :] = turned[
                sub * part : (sub + 1) * part
            ].astype(BF)
    key_value = projected[:, pairs * 128 :]
    turned = turn(key_value)
    first = lanes < HEAD
    crossed = pltpu.roll(key_value, HEAD, 1)
    turned_crossed = pltpu.roll(turned, HEAD, 1)
    one = jnp.where(first, 1.0, 0.0)
    here, there = pl.ds(base, rows), pl.ds(other_base, rows)
    k_buf[here, :] = jnp.where(first, turned, 0.0).astype(BF)
    k_buf[there, :] = jnp.where(first, 0.0, turned_crossed).astype(BF)
    v_buf[here, 0:128] = jnp.where(first, crossed, 0.0).astype(BF)
    v_buf[here, 128:256] = one.astype(BF)
    v_buf[there, 0:128] = jnp.where(first, 0.0, key_value).astype(BF)
    v_buf[there, 128:256] = (1.0 - one).astype(BF)

    def attend(sub, blocks):
        span = blocks * part
        start = pl.multiple_of((step * subs + (sub + 1 - blocks)) * part, part)
        window = pl.ds(start, span)
        other = pl.ds(pl.multiple_of(length + start, part), span)
        docs = dock_ref[:, window]
        row = lax.broadcasted_iota(jnp.int32, (part, span), 0) + (span - part)
        col = lax.broadcasted_iota(jnp.int32, (part, span), 1)
        mine = slice(sub * part, (sub + 1) * part)
        allowed = (row >= col) & (docq_ref[mine, :] == docs)
        query = q_buf[sub]
        both = None
        for i, keys in enumerate((window, other)):
            scores = lax.dot_general(query, k_buf[keys, :], NT, preferred_element_type=F32)
            for pair in range(pairs):
                cut = slice(pair * part, (pair + 1) * part)
                masked = jnp.where(allowed, scores[cut], -1e30)
                largest = jnp.max(masked, axis=-1, keepdims=True)
                p_buf[i, cut, :span] = jnp.exp(masked - largest).astype(BF)
            term = jnp.dot(p_buf[i, :, :span], v_buf[keys, :], preferred_element_type=F32)
            both = term if both is None else both + term
        result = (both[:, :128] / both[:, 128:]).astype(BF)
        for pair in range(pairs):
            h_buf[mine, pair * 128 : (pair + 1) * 128] = result[pair * part : (pair + 1) * part]

    needed = spans_ref[step]
    for blocks in range(1, SPANS + 1):

        @pl.when(needed == blocks)
        def _():
            for sub in range(subs):
                attend(sub, min(blocks + sub, SPANS))

    out_ref[...] = lax.dot_general(
        h_buf[...], out_buf[...], NT, preferred_element_type=F32
    ).astype(BF)


def attend(x, w, columns, cosine, sine, docs):
    length, width = x.shape
    inner = columns + 2 * HEAD
    rows = ATTEND_ROWS
    part = 128
    first = docs[::rows]
    begin = jnp.sum((docs[None, :] < first[:, None]).astype(jnp.int32), axis=1)
    spans = jnp.arange(length // rows, dtype=jnp.int32) * (rows // part) - begin // part + 1
    shards, depth, _ = w.shape
    total = inner + columns
    return pl.pallas_call(
        attend_kernel,
        out_shape=jax.ShapeDtypeStruct((length, width), BF),
        grid_spec=pltpu.PrefetchScalarGridSpec(
            num_scalar_prefetch=1,
            grid=(length // rows,),
            in_specs=[
                pl.BlockSpec((rows, width), lambda i, spans: (i, 0)),
                pl.BlockSpec(w.shape, lambda i, spans: (0, 0, 0)),
                pl.BlockSpec((rows, 128), lambda i, spans: (i, 0)),
                pl.BlockSpec((rows, 128), lambda i, spans: (i, 0)),
                pl.BlockSpec((rows, 1), lambda i, spans: (i, 0)),
                pl.BlockSpec((1, length), lambda i, spans: (0, 0)),
            ],
            out_specs=pl.BlockSpec((rows, width), lambda i, spans: (i, 0)),
            scratch_shapes=[
                pltpu.VMEM((width, inner), BF),
                pltpu.VMEM((width, columns), BF),
                pltpu.VMEM((rows // part, columns, 128), BF),
                pltpu.VMEM((2 * length, 128), BF),
                pltpu.VMEM((2 * length, 256), BF),
                pltpu.VMEM((2, columns, 640), BF),
                pltpu.VMEM((rows, columns), BF),
            ],
        ),
        compiler_params=pltpu.CompilerParams(vmem_limit_bytes=48 << 20),
        cost_estimate=pl.CostEstimate(
            flops=2 * length * width * total + 4 * length * 640 * columns * 2,
            bytes_accessed=2 * (2 * length * width + width * total),
            transcendentals=length * 640 * columns // HEAD,
        ),
        name="attend",
    )(spans, x, w, cosine, sine, docs.reshape(length, 1), docs.reshape(1, length))


def gather_window(normed):
    size = lax.axis_size("tensor")
    ring = size // 2
    ahead = [(t, (t // 2 + 1) % ring * 2 + t % 2) for t in range(size)]
    back = [(t, (t // 2 + ring - 1) % ring * 2 + t % 2) for t in range(size)]
    across = [(t, t ^ 1) for t in range(size)]
    half = normed.shape[0] // 2
    before = lax.ppermute(normed, "tensor", ahead)
    after = lax.ppermute(normed, "tensor", back)
    far = jnp.concatenate(
        [
            lax.ppermute(before[:half], "tensor", ahead),
            lax.ppermute(after[half:], "tensor", back),
        ],
        axis=0,
    )
    mine = jnp.stack([normed, after, far, before])
    theirs = jnp.stack([lax.ppermute(p, "tensor", across) for p in (normed, after, far, before)])
    index = lax.axis_index("tensor")
    odd = index % 2 == 1
    both = jnp.stack([jnp.where(odd, theirs, mine), jnp.where(odd, mine, theirs)], axis=1)
    return jnp.roll(both, index // 2, axis=0).reshape(-1, normed.shape[1])


def kinds(slot, rank):
    return (
        (slot == rank) & (rank >= 0) & (rank < HALF),
        (slot == rank + HALF) & (rank >= 0) & (rank < HALF),
        ((slot == 6) & (rank == 0)) | ((slot == 7) & (rank == 2)),
        (slot == 6) & (rank == 1),
        (slot == 7) & (rank == 1),
    )


def pieces(rows, tail):
    count = rows.shape[0]
    none = jnp.zeros((count, LEFT - TAIL), rows.dtype)
    left = jnp.concatenate(
        [rows[:, :LEFT], rows[:, WIDE : WIDE + LEFT], jnp.concatenate([tail, none], axis=1)], axis=0
    )
    rest = jnp.concatenate(
        [tail[:, RIGHT:], jnp.zeros((count, RIGHT - (TAIL - RIGHT)), rows.dtype)], axis=1
    )
    right = jnp.concatenate(
        [rows[:, LEFT:WIDE], rows[:, WIDE + LEFT : MAIN], tail[:, :RIGHT], rest], axis=0
    )
    return left, right


def fill(moe_in, table_ref, out_ref):
    rows = moe_in.shape[0]
    left, right = pieces(moe_in, moe_in[:, MAIN:])
    out_ref[:, :LEFT] = jnp.dot(
        table_ref[:, : 3 * rows], left, preferred_element_type=F32
    ).astype(BF)
    table = jnp.concatenate([table_ref[:, : 2 * rows], table_ref[:, 3 * rows :]], axis=1)
    out_ref[:, LEFT:] = jnp.dot(table, right, preferred_element_type=F32).astype(BF)


def dispatch_kernel(tokens_ref, attn_ref, gain_ref, table_ref, out_ref, resid_ref, in_ref):
    resid = tokens_ref[...].astype(F32) + attn_ref[...].astype(F32)
    resid_ref[...] = resid
    moe_in = rms_norm(resid, gain_ref[...]).astype(BF)
    in_ref[...] = moe_in
    fill(moe_in, table_ref, out_ref)


def refill_kernel(in_ref, table_ref, out_ref):
    fill(in_ref[...], table_ref, out_ref)


def dispatch(tokens, attn_out, gain, tables):
    rows, width = tokens.shape
    sent = jax.ShapeDtypeStruct((tables[0].shape[0], WIDE), BF)
    common = dict(
        compiler_params=pltpu.CompilerParams(vmem_limit_bytes=56 << 20),
        cost_estimate=pl.CostEstimate(
            flops=2 * sent.shape[0] * 512 * WIDE,
            bytes_accessed=2 * sent.shape[0] * (WIDE + 640) + 8 * rows * width,
            transcendentals=0,
        ),
    )
    first, resid, moe_in = pl.pallas_call(
        dispatch_kernel,
        out_shape=(
            sent,
            jax.ShapeDtypeStruct((rows, width), F32),
            jax.ShapeDtypeStruct((rows, width), BF),
        ),
        in_specs=[VMEM] * 4,
        out_specs=(VMEM,) * 3,
        name="dispatch",
        **common,
    )(tokens, attn_out, gain.reshape(1, width), tables[0])
    second = pl.pallas_call(
        refill_kernel, out_shape=sent, in_specs=[VMEM] * 2, out_specs=VMEM, name="refill", **common
    )(moe_in, tables[1])
    return first, second, resid


def after_kernel(value_ref, other_ref, out_ref):
    pass


def after(value, other):
    return pl.pallas_call(
        after_kernel,
        out_shape=jax.ShapeDtypeStruct(value.shape, value.dtype),
        in_specs=[ANY, ANY],
        out_specs=ANY,
        input_output_aliases={0: 0},
        name="after",
    )(value, other)


def expert_kernel(
    recv_ref, gate_up_ref, down_ref, pick_ref, put_ref, out_ref,
    x_buf, gate_up_buf, down_buf, both_buf, act_buf, y_buf, sems,
):
    total = x_buf.shape[0]
    tiles = [(s, min(512, WIDTH - s)) for s in range(0, WIDTH, 512)]
    copies = []
    for i, (start, size) in enumerate(tiles):
        cols = pl.ds(start, size)
        copies.append(
            pltpu.make_async_copy(gate_up_ref.at[:, cols], gate_up_buf.at[:, cols], sems.at[i])
        )
    down_copy = pltpu.make_async_copy(down_ref, down_buf, sems.at[len(tiles)])
    for copy in copies:
        copy.start()
    down_copy.start()

    blocks = recv_ref.shape[0] // 128
    few = 128 // SLOTS * HALF

    def unpack(block, carry):
        source = pl.ds(pl.multiple_of(block * 128, 128), 128)
        target = pl.ds(pl.multiple_of(block * few, few), few)
        left = jnp.dot(
            pick_ref[: 3 * few, :], recv_ref[source, :LEFT], preferred_element_type=F32
        ).astype(BF)
        right = jnp.dot(pick_ref[...], recv_ref[source, LEFT:], preferred_element_type=F32)
        first = right[3 * few : 4 * few]
        second = right[4 * few :]
        right = right.astype(BF)
        x_buf[target, :LEFT] = left[:few]
        x_buf[target, LEFT:WIDE] = right[:few]
        x_buf[target, WIDE : WIDE + LEFT] = left[few : 2 * few]
        x_buf[target, WIDE + LEFT : MAIN] = right[few : 2 * few]
        tail = left[2 * few :].astype(F32)
        x_buf[target, MAIN : MAIN + RIGHT] = (tail[:, :RIGHT] + first).astype(BF)
        x_buf[target, MAIN + RIGHT :] = (
            tail[:, RIGHT:TAIL] + second[:, : TAIL - RIGHT]
        ).astype(BF)
        return carry

    lax.fori_loop(0, blocks, unpack, 0)

    for i, (start, size) in enumerate(tiles):
        copies[i].wait()
        both_buf[:, start : start + size] = jnp.dot(
            x_buf[...], gate_up_buf[:, start : start + size], preferred_element_type=F32
        )

    def activate(m, carry):
        rows = pl.ds(pl.multiple_of(m * 64, 64), 64)
        gate = both_buf[rows, :FF]
        up = both_buf[rows, FF:]
        act_buf[rows, :] = (gate * jax.nn.sigmoid(1.702 * gate) * (up + 1.0)).astype(BF)
        return carry

    lax.fori_loop(0, total // 64, activate, 0)

    down_copy.wait()
    for start, size in tiles:
        y_buf[:, start : start + size] = jnp.dot(
            act_buf[...], down_buf[:, start : start + size], preferred_element_type=F32
        ).astype(BF)

    def pack(block, carry):
        target = pl.ds(pl.multiple_of(block * 128, 128), 128)
        source = pl.ds(pl.multiple_of(block * few, few), few)
        left, right = pieces(y_buf[source, :], y_buf[source, MAIN:])
        out_ref[target, :LEFT] = jnp.dot(
            put_ref[:, : 3 * few], left, preferred_element_type=F32
        ).astype(BF)
        put = jnp.concatenate([put_ref[:, : 2 * few], put_ref[:, 3 * few :]], axis=1)
        out_ref[target, LEFT:] = jnp.dot(put, right, preferred_element_type=F32).astype(BF)
        return carry

    lax.fori_loop(0, blocks, pack, 0)


def experts(recv, gate_up, down):
    few = 128 // SLOTS * HALF
    row = jnp.arange(few, dtype=jnp.int32)[:, None]
    source, rank = row // HALF, row % HALF
    col = jnp.arange(128, dtype=jnp.int32)[None, :]
    same = col // SLOTS == source
    pick = jnp.concatenate([(mask & same).astype(BF) for mask in kinds(col % SLOTS, rank)], axis=0)
    put = pick.T
    total = recv.shape[0] // SLOTS * HALF
    return pl.pallas_call(
        expert_kernel,
        out_shape=jax.ShapeDtypeStruct(recv.shape, BF),
        in_specs=[VMEM, ANY, ANY, VMEM, VMEM],
        out_specs=VMEM,
        scratch_shapes=[
            pltpu.VMEM((total, WIDTH), BF),
            pltpu.VMEM((WIDTH, 2 * FF), BF),
            pltpu.VMEM((FF, WIDTH), BF),
            pltpu.VMEM((total, 2 * FF), F32),
            pltpu.VMEM((total, FF), BF),
            pltpu.VMEM((total, WIDTH), BF),
            pltpu.SemaphoreType.DMA((7,)),
        ],
        compiler_params=pltpu.CompilerParams(vmem_limit_bytes=56 << 20),
        cost_estimate=pl.CostEstimate(
            flops=6 * total * FF * WIDTH,
            bytes_accessed=6 * FF * WIDTH + 4 * recv.shape[0] * WIDE,
            transcendentals=total * FF,
        ),
        name="experts",
    )(recv, gate_up, down, pick, put)


def combine_kernel(back_ref, resid_ref, coef_ref, out_ref):
    rows = resid_ref.shape[0]
    pair = 2 * rows

    def both(part, at):
        return part[at : at + rows] + part[at + rows : at + pair]

    main = jnp.dot(coef_ref[: 2 * pair, :], back_ref[...], preferred_element_type=F32)
    out_ref[:, :WIDE] = (resid_ref[:, :WIDE] + both(main, 0)).astype(out_ref.dtype)
    out_ref[:, WIDE:MAIN] = (resid_ref[:, WIDE:MAIN] + both(main, pair)).astype(out_ref.dtype)
    left = jnp.dot(
        coef_ref[2 * pair : 3 * pair, :], back_ref[:, :LEFT], preferred_element_type=F32
    )
    right = jnp.dot(coef_ref[3 * pair :, :], back_ref[:, LEFT:], preferred_element_type=F32)
    tail = both(left, 0)
    out_ref[:, MAIN : MAIN + RIGHT] = (
        resid_ref[:, MAIN : MAIN + RIGHT] + (tail[:, :RIGHT] + both(right, 0))
    ).astype(out_ref.dtype)
    out_ref[:, MAIN + RIGHT :] = (
        resid_ref[:, MAIN + RIGHT :]
        + (tail[:, RIGHT:TAIL] + both(right, pair)[:, : TAIL - RIGHT])
    ).astype(out_ref.dtype)


def combine(back, resid, coef, dtype):
    rows, width = resid.shape
    return pl.pallas_call(
        combine_kernel,
        out_shape=jax.ShapeDtypeStruct((rows, width), dtype),
        in_specs=[VMEM] * 3,
        out_specs=VMEM,
        compiler_params=pltpu.CompilerParams(vmem_limit_bytes=24 << 20),
        cost_estimate=pl.CostEstimate(
            flops=4 * back.shape[0] * rows * (MAIN + 2 * WIDE),
            bytes_accessed=2 * back.shape[0] * (WIDE + 1280) + 8 * rows * width,
            transcendentals=0,
        ),
        name="combine",
    )(back, resid, coef)


def routing(expert_ids, gate_weights, experts_count):
    rows = expert_ids.shape[0]
    names = jnp.arange(experts_count, dtype=jnp.int32)
    named = expert_ids.T[:, None, :] == names[None, :, None]
    hit = jnp.any(named, axis=0)
    share = gate_weights / jnp.sum(gate_weights, axis=-1, keepdims=True)
    weight = jnp.sum(jnp.where(named, share.T[:, None, :], 0.0), axis=0)
    index = jnp.arange(rows, dtype=jnp.int32)
    earlier = (index[:, None] < index[None, :]).astype(BF)
    rank = jnp.dot(hit.astype(BF), earlier, preferred_element_type=F32).astype(jnp.int32)
    rank = jnp.where(hit, rank, -CAP)
    size = experts_count * SLOTS
    spread = jnp.broadcast_to(rank[:, None, :], (experts_count, SLOTS, rows)).reshape(size, rows)
    slot = lax.broadcasted_iota(jnp.int32, (size, rows), 0) % SLOTS
    weight = jnp.broadcast_to(weight[:, None, :], (experts_count, SLOTS, rows)).reshape(size, rows)
    high = weight.astype(BF)
    low = (weight - high.astype(F32)).astype(BF)
    none = jnp.zeros((), BF)
    tables, coefs = [], []
    for part in range(CAP // HALF):
        masks = kinds(slot, spread - part * HALF)
        tables.append(jnp.concatenate([mask.astype(BF) for mask in masks], axis=1))
        coefs.append(
            jnp.concatenate(
                [jnp.where(mask, term, none) for mask in masks for term in (high, low)], axis=1
            ).T
        )
    return tables, coefs


def body(
    tokens,
    positions,
    doc_ids,
    w_query,
    key_weight,
    value_weight,
    w_out,
    attn_gain,
    moe_gain,
    expert_ids,
    gate_weights,
    w_gate_up,
    w_down,
):
    normed = rms_norm(tokens.astype(F32), attn_gain).astype(BF)
    joined = jnp.concatenate([w_query, key_weight, value_weight, w_out.T], axis=1)
    weights = lax.all_gather(joined, "dp", axis=0, tiled=False)
    window = gather_window(normed)

    half = HEAD // 2
    freq = jnp.exp(jnp.arange(half, dtype=F32) * (-2.0 * math.log(150000.0) / HEAD))
    angle = positions[0].astype(F32)[:, None] * freq[None, :]
    cosine, sine = jnp.cos(angle), jnp.sin(angle)
    cosine = jnp.concatenate([cosine] * 4, axis=1)
    sine = jnp.concatenate([-sine, sine] * 2, axis=1)
    experts_count = lax.axis_size("dp") * lax.axis_size("tensor")
    tables, coef = routing(expert_ids, gate_weights, experts_count)

    partial_sums = attend(window, weights, w_query.shape[1], cosine, sine, doc_ids[0])
    attn_out = lax.psum_scatter(partial_sums, "tensor", scatter_dimension=0, tiled=True)
    first, second, resid = dispatch(tokens, attn_out, moe_gain, tables)
    gate_up, down = w_gate_up[0], w_down[0]

    def exchange(blocks):
        return lax.all_to_all(blocks, ("dp", "tensor"), split_axis=0, concat_axis=0, tiled=True)

    first_in = exchange(first)
    second_in = exchange(after(second, first_in))
    first_back = exchange(experts(first_in, gate_up, down))
    second_back = exchange(experts(second_in, gate_up, down))
    mixed = combine(first_back, resid, coef[0], F32)
    return combine(second_back, mixed, coef[1], BF)


def solution(mesh):
    placed = (
        P(("dp", "tensor"), None),
        P("dp", None),
        P("dp", None),
        P("dp", "tensor"),
        P("dp", "tensor"),
        P("dp", "tensor"),
        P("tensor", "dp"),
        P(),
        P(),
        P(("dp", "tensor"), None),
        P(("dp", "tensor"), None),
        P(("dp", "tensor"), None, None),
        P(("dp", "tensor"), None, None),
    )
    return jax.shard_map(
        body, mesh=mesh, in_specs=placed, out_specs=P(("dp", "tensor"), None), check_vma=False
    )
```

```python
import math

import jax
import jax.numpy as jnp
from jax import lax
from jax.experimental import pallas as pl
from jax.experimental.pallas import tpu as pltpu
from jax.sharding import PartitionSpec as P

HEAD = 64
WIDTH = 2880
FF = 1440
CAP = 6
ATTEND_ROWS = 256
SPANS = 5
HALF = 3
SLOTS = 8
WIDE = 1152
LEFT = 640
RIGHT = WIDE - LEFT
MAIN = 2 * WIDE
TAIL = WIDTH - MAIN
BF = jnp.bfloat16
F32 = jnp.float32
NT = (((1,), (1,)), ((), ()))
VMEM = pl.BlockSpec(memory_space=pltpu.VMEM)
ANY = pl.BlockSpec(memory_space=pl.ANY)


def rms_norm(value_rows, gain):
    mean_square = jnp.mean(value_rows * value_rows, axis=-1, keepdims=True)
    return value_rows * lax.rsqrt(mean_square + 1e-05) * gain


def attend_kernel(
    x_ref, w_ref, cos_ref, sin_ref, docq_ref, dock_ref, out_ref,
    in_buf, out_buf, q_buf, k_buf, v_buf, p_buf, h_buf,
):
    step = pl.program_id(0)
    rows = x_ref.shape[0]
    part = 128
    subs = rows // part
    length = k_buf.shape[0] // 2
    pairs = h_buf.shape[1] // 128
    inner = in_buf.shape[1]
    base = pl.multiple_of(step * rows, rows)
    other_base = pl.multiple_of(length + step * rows, rows)

    @pl.when(step == 0)
    def _():
        shards, depth, _ = w_ref.shape
        for i in range(0, shards, 4):
            four = slice(i * depth, (i + 4) * depth)
            for at in range(0, w_ref.shape[2], 128):
                block = jnp.concatenate(
                    [w_ref[i + j, :, at : at + 128].astype(F32) for j in range(4)], axis=0
                ).astype(BF)
                if at < inner:
                    in_buf[four, at : at + 128] = block
                else:
                    out_buf[four, at - inner : at - inner + 128] = block

    projected = jnp.dot(x_ref[...], in_buf[...], preferred_element_type=F32)
    lanes = lax.broadcasted_iota(jnp.int32, (rows, 128), 1)
    low = (lanes % HEAD) < HEAD // 2
    cosine = cos_ref[...]
    sine = sin_ref[...]

    def turn(pair):
        swapped = jnp.where(
            low, pltpu.roll(pair, 128 - HEAD // 2, 1), pltpu.roll(pair, HEAD // 2, 1)
        )
        return pair * cosine + swapped * sine

    for pair in range(pairs):
        turned = turn(projected[:, pair * 128 : pair * 128 + 128]) * HEAD ** (-0.5)
        for sub in range(subs):
            q_buf[sub, pair * part : (pair + 1) * part, :] = turned[
                sub * part : (sub + 1) * part
            ].astype(BF)
    key_value = projected[:, pairs * 128 :]
    turned = turn(key_value)
    first = lanes < HEAD
    crossed = pltpu.roll(key_value, HEAD, 1)
    turned_crossed = pltpu.roll(turned, HEAD, 1)
    one = jnp.where(first, 1.0, 0.0)
    here, there = pl.ds(base, rows), pl.ds(other_base, rows)
    k_buf[here, :] = jnp.where(first, turned, 0.0).astype(BF)
    k_buf[there, :] = jnp.where(first, 0.0, turned_crossed).astype(BF)
    v_buf[here, 0:128] = jnp.where(first, crossed, 0.0).astype(BF)
    v_buf[here, 128:256] = one.astype(BF)
    v_buf[there, 0:128] = jnp.where(first, 0.0, key_value).astype(BF)
    v_buf[there, 128:256] = (1.0 - one).astype(BF)

    def attend(sub, blocks):
        span = blocks * part
        start = pl.multiple_of((step * subs + (sub + 1 - blocks)) * part, part)
        window = pl.ds(start, span)
        other = pl.ds(pl.multiple_of(length + start, part), span)
        docs = dock_ref[:, window]
        row = lax.broadcasted_iota(jnp.int32, (part, span), 0) + (span - part)
        col = lax.broadcasted_iota(jnp.int32, (part, span), 1)
        mine = slice(sub * part, (sub + 1) * part)
        allowed = (row >= col) & (docq_ref[mine, :] == docs)
        query = q_buf[sub]
        both = None
        for i, keys in enumerate((window, other)):
            scores = lax.dot_general(query, k_buf[keys, :], NT, preferred_element_type=F32)
            for pair in range(pairs):
                cut = slice(pair * part, (pair + 1) * part)
                masked = jnp.where(allowed, scores[cut], -1e30)
                largest = jnp.max(masked, axis=-1, keepdims=True)
                p_buf[i, cut, :span] = jnp.exp(masked - largest).astype(BF)
            term = jnp.dot(p_buf[i, :, :span], v_buf[keys, :], preferred_element_type=F32)
            both = term if both is None else both + term
        result = (both[:, :128] / both[:, 128:]).astype(BF)
        for pair in range(pairs):
            h_buf[mine, pair * 128 : (pair + 1) * 128] = result[pair * part : (pair + 1) * part]

    for turns in range(2):

        @pl.when(step == turns)
        def _():
            for sub in range(subs):
                attend(sub, turns * subs + sub + 1)

    @pl.when(step >= 2)
    def _():
        for sub in range(subs):
            attend(sub, SPANS)

    out_ref[...] = lax.dot_general(
        h_buf[...], out_buf[...], NT, preferred_element_type=F32
    ).astype(BF)


def attend(x, w, columns, cosine, sine, docs):
    length, width = x.shape
    inner = columns + 2 * HEAD
    rows = ATTEND_ROWS
    part = 128
    shards, depth, _ = w.shape
    total = inner + columns
    return pl.pallas_call(
        attend_kernel,
        out_shape=jax.ShapeDtypeStruct((length, width), BF),
        grid=(length // rows,),
        in_specs=[
            pl.BlockSpec((rows, width), lambda i: (i, 0)),
            pl.BlockSpec(w.shape, lambda i: (0, 0, 0)),
            pl.BlockSpec((rows, 128), lambda i: (i, 0)),
            pl.BlockSpec((rows, 128), lambda i: (i, 0)),
            pl.BlockSpec((rows, 1), lambda i: (i, 0)),
            pl.BlockSpec((1, length), lambda i: (0, 0)),
        ],
        out_specs=pl.BlockSpec((rows, width), lambda i: (i, 0)),
        scratch_shapes=[
            pltpu.VMEM((width, inner), BF),
            pltpu.VMEM((width, columns), BF),
            pltpu.VMEM((rows // part, columns, 128), BF),
            pltpu.VMEM((2 * length, 128), BF),
            pltpu.VMEM((2 * length, 256), BF),
            pltpu.VMEM((2, columns, 640), BF),
            pltpu.VMEM((rows, columns), BF),
        ],
        compiler_params=pltpu.CompilerParams(vmem_limit_bytes=48 << 20),
        cost_estimate=pl.CostEstimate(
            flops=2 * length * width * total + 4 * length * 640 * columns * 2,
            bytes_accessed=2 * (2 * length * width + width * total),
            transcendentals=length * 640 * columns // HEAD,
        ),
        name="attend",
    )(x, w, cosine, sine, docs.reshape(length, 1), docs.reshape(1, length))


def gather_window(normed):
    size = lax.axis_size("tensor")
    ring = size // 2
    ahead = [(t, (t // 2 + 1) % ring * 2 + t % 2) for t in range(size)]
    back = [(t, (t // 2 + ring - 1) % ring * 2 + t % 2) for t in range(size)]
    across = [(t, t ^ 1) for t in range(size)]
    half = normed.shape[0] // 2
    before = lax.ppermute(normed, "tensor", ahead)
    after = lax.ppermute(normed, "tensor", back)
    far = jnp.concatenate(
        [
            lax.ppermute(before[:half], "tensor", ahead),
            lax.ppermute(after[half:], "tensor", back),
        ],
        axis=0,
    )
    mine = jnp.stack([normed, after, far, before])
    theirs = jnp.stack([lax.ppermute(p, "tensor", across) for p in (normed, after, far, before)])
    index = lax.axis_index("tensor")
    odd = index % 2 == 1
    both = jnp.stack([jnp.where(odd, theirs, mine), jnp.where(odd, mine, theirs)], axis=1)
    return jnp.roll(both, index // 2, axis=0).reshape(-1, normed.shape[1])


def kinds(slot, rank):
    return (
        (slot == rank) & (rank >= 0) & (rank < HALF),
        (slot == rank + HALF) & (rank >= 0) & (rank < HALF),
        ((slot == 6) & (rank == 0)) | ((slot == 7) & (rank == 2)),
        (slot == 6) & (rank == 1),
        (slot == 7) & (rank == 1),
    )


def pieces(rows, tail):
    count = rows.shape[0]
    none = jnp.zeros((count, LEFT - TAIL), rows.dtype)
    left = jnp.concatenate(
        [rows[:, :LEFT], rows[:, WIDE : WIDE + LEFT], jnp.concatenate([tail, none], axis=1)], axis=0
    )
    rest = jnp.concatenate(
        [tail[:, RIGHT:], jnp.zeros((count, RIGHT - (TAIL - RIGHT)), rows.dtype)], axis=1
    )
    right = jnp.concatenate(
        [rows[:, LEFT:WIDE], rows[:, WIDE + LEFT : MAIN], tail[:, :RIGHT], rest], axis=0
    )
    return left, right


def fill(moe_in, table_ref, out_ref):
    rows = moe_in.shape[0]
    left, right = pieces(moe_in, moe_in[:, MAIN:])
    out_ref[:, :LEFT] = jnp.dot(
        table_ref[:, : 3 * rows], left, preferred_element_type=F32
    ).astype(BF)
    table = jnp.concatenate([table_ref[:, : 2 * rows], table_ref[:, 3 * rows :]], axis=1)
    out_ref[:, LEFT:] = jnp.dot(table, right, preferred_element_type=F32).astype(BF)


def dispatch_kernel(tokens_ref, attn_ref, gain_ref, table_ref, out_ref, resid_ref, in_ref):
    resid = tokens_ref[...].astype(F32) + attn_ref[...].astype(F32)
    resid_ref[...] = resid
    moe_in = rms_norm(resid, gain_ref[...]).astype(BF)
    in_ref[...] = moe_in
    fill(moe_in, table_ref, out_ref)


def refill_kernel(in_ref, table_ref, out_ref):
    fill(in_ref[...], table_ref, out_ref)


def dispatch(tokens, attn_out, gain, tables):
    rows, width = tokens.shape
    sent = jax.ShapeDtypeStruct((tables[0].shape[0], WIDE), BF)
    common = dict(
        compiler_params=pltpu.CompilerParams(vmem_limit_bytes=56 << 20),
        cost_estimate=pl.CostEstimate(
            flops=2 * sent.shape[0] * 512 * WIDE,
            bytes_accessed=2 * sent.shape[0] * (WIDE + 640) + 8 * rows * width,
            transcendentals=0,
        ),
    )
    first, resid, moe_in = pl.pallas_call(
        dispatch_kernel,
        out_shape=(
            sent,
            jax.ShapeDtypeStruct((rows, width), F32),
            jax.ShapeDtypeStruct((rows, width), BF),
        ),
        in_specs=[VMEM] * 4,
        out_specs=(VMEM,) * 3,
        name="dispatch",
        **common,
    )(tokens, attn_out, gain.reshape(1, width), tables[0])
    second = pl.pallas_call(
        refill_kernel, out_shape=sent, in_specs=[VMEM] * 2, out_specs=VMEM, name="refill", **common
    )(moe_in, tables[1])
    return first, second, resid


def after_kernel(value_ref, other_ref, out_ref):
    pass


def after(value, other):
    return pl.pallas_call(
        after_kernel,
        out_shape=jax.ShapeDtypeStruct(value.shape, value.dtype),
        in_specs=[ANY, ANY],
        out_specs=ANY,
        input_output_aliases={0: 0},
        name="after",
    )(value, other)


def expert_kernel(
    recv_ref, gate_up_ref, down_ref, pick_ref, put_ref, out_ref,
    x_buf, gate_up_buf, down_buf, both_buf, act_buf, y_buf, sems,
):
    total = x_buf.shape[0]
    tiles = [(s, min(512, WIDTH - s)) for s in range(0, WIDTH, 512)]
    copies = []
    for i, (start, size) in enumerate(tiles):
        cols = pl.ds(start, size)
        copies.append(
            pltpu.make_async_copy(gate_up_ref.at[:, cols], gate_up_buf.at[:, cols], sems.at[i])
        )
    down_copy = pltpu.make_async_copy(down_ref, down_buf, sems.at[len(tiles)])
    for copy in copies:
        copy.start()
    down_copy.start()

    blocks = recv_ref.shape[0] // 128
    few = 128 // SLOTS * HALF

    def unpack(block, carry):
        source = pl.ds(pl.multiple_of(block * 128, 128), 128)
        target = pl.ds(pl.multiple_of(block * few, few), few)
        left = jnp.dot(
            pick_ref[: 3 * few, :], recv_ref[source, :LEFT], preferred_element_type=F32
        ).astype(BF)
        right = jnp.dot(pick_ref[...], recv_ref[source, LEFT:], preferred_element_type=F32)
        first = right[3 * few : 4 * few]
        second = right[4 * few :]
        right = right.astype(BF)
        x_buf[target, :LEFT] = left[:few]
        x_buf[target, LEFT:WIDE] = right[:few]
        x_buf[target, WIDE : WIDE + LEFT] = left[few : 2 * few]
        x_buf[target, WIDE + LEFT : MAIN] = right[few : 2 * few]
        tail = left[2 * few :].astype(F32)
        x_buf[target, MAIN : MAIN + RIGHT] = (tail[:, :RIGHT] + first).astype(BF)
        x_buf[target, MAIN + RIGHT :] = (
            tail[:, RIGHT:TAIL] + second[:, : TAIL - RIGHT]
        ).astype(BF)
        return carry

    lax.fori_loop(0, blocks, unpack, 0)

    for i, (start, size) in enumerate(tiles):
        copies[i].wait()
        both_buf[:, start : start + size] = jnp.dot(
            x_buf[...], gate_up_buf[:, start : start + size], preferred_element_type=F32
        )

    def activate(m, carry):
        rows = pl.ds(pl.multiple_of(m * 64, 64), 64)
        gate = both_buf[rows, :FF]
        up = both_buf[rows, FF:]
        act_buf[rows, :] = (gate * jax.nn.sigmoid(1.702 * gate) * (up + 1.0)).astype(BF)
        return carry

    lax.fori_loop(0, total // 64, activate, 0)

    down_copy.wait()
    for start, size in tiles:
        y_buf[:, start : start + size] = jnp.dot(
            act_buf[...], down_buf[:, start : start + size], preferred_element_type=F32
        ).astype(BF)

    def pack(block, carry):
        target = pl.ds(pl.multiple_of(block * 128, 128), 128)
        source = pl.ds(pl.multiple_of(block * few, few), few)
        left, right = pieces(y_buf[source, :], y_buf[source, MAIN:])
        out_ref[target, :LEFT] = jnp.dot(
            put_ref[:, : 3 * few], left, preferred_element_type=F32
        ).astype(BF)
        put = jnp.concatenate([put_ref[:, : 2 * few], put_ref[:, 3 * few :]], axis=1)
        out_ref[target, LEFT:] = jnp.dot(put, right, preferred_element_type=F32).astype(BF)
        return carry

    lax.fori_loop(0, blocks, pack, 0)


def experts(recv, gate_up, down):
    few = 128 // SLOTS * HALF
    row = jnp.arange(few, dtype=jnp.int32)[:, None]
    source, rank = row // HALF, row % HALF
    col = jnp.arange(128, dtype=jnp.int32)[None, :]
    same = col // SLOTS == source
    pick = jnp.concatenate([(mask & same).astype(BF) for mask in kinds(col % SLOTS, rank)], axis=0)
    put = pick.T
    total = recv.shape[0] // SLOTS * HALF
    return pl.pallas_call(
        expert_kernel,
        out_shape=jax.ShapeDtypeStruct(recv.shape, BF),
        in_specs=[VMEM, ANY, ANY, VMEM, VMEM],
        out_specs=VMEM,
        scratch_shapes=[
            pltpu.VMEM((total, WIDTH), BF),
            pltpu.VMEM((WIDTH, 2 * FF), BF),
            pltpu.VMEM((FF, WIDTH), BF),
            pltpu.VMEM((total, 2 * FF), F32),
            pltpu.VMEM((total, FF), BF),
            pltpu.VMEM((total, WIDTH), BF),
            pltpu.SemaphoreType.DMA((7,)),
        ],
        compiler_params=pltpu.CompilerParams(vmem_limit_bytes=46 << 20),
        cost_estimate=pl.CostEstimate(
            flops=6 * total * FF * WIDTH,
            bytes_accessed=6 * FF * WIDTH + 4 * recv.shape[0] * WIDE,
            transcendentals=total * FF,
        ),
        name="experts",
    )(recv, gate_up, down, pick, put)


def combine_kernel(back_ref, resid_ref, coef_ref, out_ref):
    rows = resid_ref.shape[0]
    pair = 2 * rows

    def both(part, at):
        return part[at : at + rows] + part[at + rows : at + pair]

    main = jnp.dot(coef_ref[: 2 * pair, :], back_ref[...], preferred_element_type=F32)
    out_ref[:, :WIDE] = (resid_ref[:, :WIDE] + both(main, 0)).astype(out_ref.dtype)
    out_ref[:, WIDE:MAIN] = (resid_ref[:, WIDE:MAIN] + both(main, pair)).astype(out_ref.dtype)
    left = jnp.dot(
        coef_ref[2 * pair : 3 * pair, :], back_ref[:, :LEFT], preferred_element_type=F32
    )
    right = jnp.dot(coef_ref[3 * pair :, :], back_ref[:, LEFT:], preferred_element_type=F32)
    tail = both(left, 0)
    out_ref[:, MAIN : MAIN + RIGHT] = (
        resid_ref[:, MAIN : MAIN + RIGHT] + (tail[:, :RIGHT] + both(right, 0))
    ).astype(out_ref.dtype)
    out_ref[:, MAIN + RIGHT :] = (
        resid_ref[:, MAIN + RIGHT :]
        + (tail[:, RIGHT:TAIL] + both(right, pair)[:, : TAIL - RIGHT])
    ).astype(out_ref.dtype)


def combine(back, resid, coef, dtype):
    rows, width = resid.shape
    return pl.pallas_call(
        combine_kernel,
        out_shape=jax.ShapeDtypeStruct((rows, width), dtype),
        in_specs=[VMEM] * 3,
        out_specs=VMEM,
        compiler_params=pltpu.CompilerParams(vmem_limit_bytes=24 << 20),
        cost_estimate=pl.CostEstimate(
            flops=4 * back.shape[0] * rows * (MAIN + 2 * WIDE),
            bytes_accessed=2 * back.shape[0] * (WIDE + 1280) + 8 * rows * width,
            transcendentals=0,
        ),
        name="combine",
    )(back, resid, coef)


def routing(expert_ids, gate_weights, experts_count):
    rows = expert_ids.shape[0]
    names = jnp.arange(experts_count, dtype=jnp.int32)
    named = expert_ids.T[:, None, :] == names[None, :, None]
    hit = jnp.any(named, axis=0)
    share = gate_weights / jnp.sum(gate_weights, axis=-1, keepdims=True)
    weight = jnp.sum(jnp.where(named, share.T[:, None, :], 0.0), axis=0)
    index = jnp.arange(rows, dtype=jnp.int32)
    earlier = (index[:, None] < index[None, :]).astype(BF)
    rank = jnp.dot(hit.astype(BF), earlier, preferred_element_type=F32).astype(jnp.int32)
    rank = jnp.where(hit, rank, -CAP)
    size = experts_count * SLOTS
    spread = jnp.broadcast_to(rank[:, None, :], (experts_count, SLOTS, rows)).reshape(size, rows)
    slot = lax.broadcasted_iota(jnp.int32, (size, rows), 0) % SLOTS
    weight = jnp.broadcast_to(weight[:, None, :], (experts_count, SLOTS, rows)).reshape(size, rows)
    high = weight.astype(BF)
    low = (weight - high.astype(F32)).astype(BF)
    none = jnp.zeros((), BF)
    tables, coefs = [], []
    for part in range(CAP // HALF):
        masks = kinds(slot, spread - part * HALF)
        tables.append(jnp.concatenate([mask.astype(BF) for mask in masks], axis=1))
        coefs.append(
            jnp.concatenate(
                [jnp.where(mask, term, none) for mask in masks for term in (high, low)], axis=1
            ).T
        )
    return tables, coefs


def body(
    tokens,
    positions,
    doc_ids,
    w_query,
    key_weight,
    value_weight,
    w_out,
    attn_gain,
    moe_gain,
    expert_ids,
    gate_weights,
    w_gate_up,
    w_down,
):
    normed = rms_norm(tokens.astype(F32), attn_gain).astype(BF)
    joined = jnp.concatenate([w_query, key_weight, value_weight, w_out.T], axis=1)
    weights = lax.all_gather(joined, "dp", axis=0, tiled=False)
    window = gather_window(normed)

    half = HEAD // 2
    freq = jnp.exp(jnp.arange(half, dtype=F32) * (-2.0 * math.log(150000.0) / HEAD))
    angle = positions[0].astype(F32)[:, None] * freq[None, :]
    cosine, sine = jnp.cos(angle), jnp.sin(angle)
    cosine = jnp.concatenate([cosine] * 4, axis=1)
    sine = jnp.concatenate([-sine, sine] * 2, axis=1)
    experts_count = lax.axis_size("dp") * lax.axis_size("tensor")
    tables, coef = routing(expert_ids, gate_weights, experts_count)

    partial_sums = attend(window, weights, w_query.shape[1], cosine, sine, doc_ids[0])
    attn_out = lax.psum_scatter(partial_sums, "tensor", scatter_dimension=0, tiled=True)
    first, second, resid = dispatch(tokens, attn_out, moe_gain, tables)
    gate_up, down = w_gate_up[0], w_down[0]

    def exchange(blocks):
        return lax.all_to_all(blocks, ("dp", "tensor"), split_axis=0, concat_axis=0, tiled=True)

    first_in = exchange(first)
    second_in = exchange(after(second, first_in))
    first_back = exchange(experts(first_in, gate_up, down))
    second_back = exchange(experts(second_in, gate_up, down))
    mixed = combine(first_back, resid, coef[0], F32)
    return combine(second_back, mixed, coef[1], BF)


def solution(mesh):
    placed = (
        P(("dp", "tensor"), None),
        P("dp", None),
        P("dp", None),
        P("dp", "tensor"),
        P("dp", "tensor"),
        P("dp", "tensor"),
        P("tensor", "dp"),
        P(),
        P(),
        P(("dp", "tensor"), None),
        P(("dp", "tensor"), None),
        P(("dp", "tensor"), None, None),
        P(("dp", "tensor"), None, None),
    )
    return jax.shard_map(
        body, mesh=mesh, in_specs=placed, out_specs=P(("dp", "tensor"), None), check_vma=False
    )
```
